128 devices in a mesh: ix: 4 (over z), iy: 4 (over x), depth: 8 (over y, core).
Axes of the slice: x: 4, y: 4, z: 4, core: 2. Of those that a mesh axis runs over, the one named last changes fastest.
Arguments:
- density: bfloat16 [512, 1024, 1024], P('depth', 'ix', 'iy'), may hold values from -4 to 4
Outputs:
- image: float32 [4, 1024, 1024], P(None, ('ix', 'depth'), 'iy')
The draws below stay inside these ranges and needn't reach their ends.
All inputs are finite; a program needn't handle non-finite values.
Results may differ from the reference program's by a relative error of at most 0.0003.
Values may be sent and summed in bfloat16 or wider, within the bound.
A program may use at most 128 MiB of HBM per device.

```python
import jax
import jax.numpy as jnp
from jax import lax

NZ = 512
NX = 1024
NY = 1024


def steps_of(stream_key, extent, pieces, least, top_value):
    factor_of = 1.0
    for axis_at, shards_of in pieces:
        draws = jax.random.uniform(jax.random.fold_in(jax.random.fold_in(stream_key, 6), axis_at), (shards_of,), jnp.float32, least / len(pieces), top_value / len(pieces))
        factor_of = factor_of * jnp.repeat(jnp.exp(draws), extent[axis_at] // shards_of).reshape((-1,) + (1,) * (len(extent) - 1 - axis_at))
    return factor_of


def gaussian(own_key, dims, spread, reach, cuts=(), held_as=jnp.bfloat16):
    result = jax.random.normal(own_key, dims, jnp.float32) * spread
    if len(cuts) > 0:
        result = steps_of(own_key, dims, cuts, -0.22, 0.18) * result
    return jnp.clip(result, min=-reach, max=reach).astype(held_as)


def setup_inputs(seed: int = 0) -> dict:
    keys = jax.random.split(jax.random.key(seed), 2)
    return {
        "density": gaussian(keys[0], (NZ, NX, NY), 1.0, 4.0, ((0, 8), (1, 4), (2, 4))),
    }


def offset_view(volume, shift_z, shift_x, shift_y):
    size_z = volume.shape[0] - 4
    size_x = volume.shape[1] - 4
    size_y = volume.shape[2] - 4
    return volume[2 + shift_z:2 + shift_z + size_z, 2 + shift_x:2 + shift_x + size_x, 2 + shift_y:2 + shift_y + size_y]

def derivative(volume, direction_unit):
    samples = [offset_view(volume, *[k * u for u in direction_unit]) for k in (2, 1, -1, -2)]
    return (8.0 * (samples[1] - samples[2]) - (samples[0] - samples[3])) / 12.0

def shade_brick(volume, spacing):
    center = offset_view(volume, 0, 0, 0)
    slope_z = derivative(volume, (1, 0, 0))
    slope_x = derivative(volume, (0, 1, 0))
    slope_y = derivative(volume, (0, 0, 1))
    facing = jnp.abs(0.48 * slope_z + 0.6 * slope_x + 0.64 * slope_y) * lax.rsqrt(slope_z * slope_z + slope_x * slope_x + slope_y * slope_y + 1.0)
    brightness = 0.3 + 0.7 * facing
    extinct = 0.2 * jnp.cosh(2.0 * center)
    cell_alpha = 1.0 - jnp.exp(-spacing * extinct)
    optical_before = jnp.cumsum(extinct, axis=0) - extinct
    weights = jnp.exp(-spacing * optical_before) * cell_alpha * brightness
    channel_red = lax.optimization_barrier(jnp.sum(weights * jax.nn.sigmoid(2.0 * center), axis=0))
    channel_green = lax.optimization_barrier(jnp.sum(weights * jnp.exp(-center * center), axis=0))
    channel_blue = lax.optimization_barrier(jnp.sum(weights * jax.nn.sigmoid(-2.0 * center), axis=0))
    optical_depth = spacing * lax.optimization_barrier(jnp.sum(extinct, axis=0))
    return (channel_red, channel_green, channel_blue, optical_depth)

def reference(density):
    depth_cells = density.shape[0]
    width_cells = density.shape[1]
    height_cells = density.shape[2]
    spacing = 1.0 / depth_cells
    padded = jnp.pad(density, 2)

    def render_block(block_index):
        volume = lax.dynamic_slice_in_dim(padded, block_index * 16, 20, 1).astype(jnp.float32)
        channel_red, channel_green, channel_blue, optical_depth = shade_brick(volume, spacing)
        return jnp.stack([channel_red, channel_green, channel_blue, 1.0 - jnp.exp(-optical_depth)])
    blocks = lax.map(render_block, jnp.arange(width_cells // 16, dtype=jnp.int32))
    return blocks.transpose(1, 0, 2, 3).reshape(4, width_cells, height_cells)
```

```python
import jax
import jax.numpy as jnp
import numpy as np
from jax import lax
from jax.experimental import pallas as pl
from jax.experimental.pallas import tpu as pltpu
from jax.sharding import PartitionSpec as P

MESH = pl.DeviceIdType.MESH
F32, BF16 = jnp.float32, jnp.bfloat16
Z, X, Y = 64, 256, 256
DEPTH = 8
ROWS = X // DEPTH
EDGE = 16
NZ = 512
EXP2_2D = float(2.0 * np.log2(np.e))
EXP2_K = float(-0.1 * np.log2(np.e) / NZ)
EXP2_SQ = float(-np.log2(np.e))
BASE = 25.0 * 0.3 / 0.7
TAPS = ((1, 8.0), (-1, -8.0), (2, -1.0), (-2, 1.0))


def along_y():
    inner = np.zeros((Y, Y), np.float32)
    outer = np.zeros((256, Y), np.float32)
    for y in range(Y):
        for step, tap in TAPS:
            at = y + step
            if 0 <= at < Y:
                inner[at, y] = tap
            elif at < 0:
                outer[[2 * z + at + 2 for z in range(Z)], y] = tap
            else:
                outer[[128 + 2 * z + at - Y for z in range(Z)], y] = tap
    return np.concatenate([inner, outer])


def along_zx():
    start = (0, 32, 64 + 16, 128 + 16, 192, 224)
    out = np.zeros((3, 2, ROWS, 256), np.float32)
    for layer in range(2):
        for row in range(ROWS):
            for step, tap in TAPS:
                across = start[layer + 2] + row + step
                behind = start[layer + 2 + step] + row
                out[0, layer, row, across] += tap
                out[1, layer, row, behind] += tap
                out[2, layer, row, across] += 15 * tap
                out[2, layer, row, behind] += 12 * tap
    return out.reshape(6 * ROWS, 256)


def pick_columns():
    out = np.zeros((Y, 256), np.float32)
    for lane in range(256):
        out[(0 if lane < 128 else Y - 2) + lane % 2, lane] = 1
    return out


def pick_rows():
    out = np.zeros((2, 16, 128), np.float32)
    for layer in range(8):
        for row in range(2):
            out[0, 2 * layer + row, 16 * layer + row] = 1
            out[1, 2 * layer + row, 16 * layer + 14 + row] = 1
    return out


def kernel(
    x_ref, y_mat, zx_mat, col_mat, row_mat, unrow_mat, out_ref,
    cells, halo, pack, row_pack, row_halo, parts, got, gy0, g0, gy1, g1,
    load_sem, z_send, z_recv, x_send, x_recv, y_send, y_recv, send_sem, recv_sem,
):
    me = lax.axis_index("depth")
    ix, iy = lax.axis_index("ix"), lax.axis_index("iy")
    n_ix, n_iy = lax.axis_size("ix"), lax.axis_size("iy")
    front, back = me > 0, me < DEPTH - 1
    up, down = ix > 0, ix < n_ix - 1
    left, right = iy > 0, iy < n_iy - 1

    def load(b):
        rows = pl.ds(pl.multiple_of(ROWS * b, ROWS), ROWS)
        inner = pl.ds(pl.multiple_of(EDGE + ROWS * b, EDGE), ROWS)
        return pltpu.make_async_copy(x_ref.at[:, rows], cells.at[pl.ds(2, Z), inner], load_sem.at[b])

    for b in range(DEPTH):
        load(b).start()

    barrier = pltpu.get_barrier_semaphore()
    for step in range(1, DEPTH):
        pl.semaphore_signal(barrier, inc=1, device_id={"depth": lax.rem(me + step, DEPTH)}, device_id_type=MESH)
    for axis, at, count in (("ix", ix, n_ix), ("iy", iy, n_iy)):
        for step in (1, count - 1):
            pl.semaphore_signal(barrier, inc=1, device_id={axis: lax.rem(at + step, count)}, device_id_type=MESH)
    pl.semaphore_wait(barrier, DEPTH - 1 + 4)

    def remote(src, dst, sems, recvs, k, axis, to):
        return pltpu.make_async_remote_copy(
            src_ref=src, dst_ref=dst, send_sem=sems.at[k], recv_sem=recvs.at[k],
            device_id={axis: to}, device_id_type=MESH,
        )

    body = pl.ds(EDGE, X)
    z_up = remote(x_ref.at[pl.ds(Z - 2, 2)], cells.at[pl.ds(0, 2), body], z_send, z_recv, 0, "depth", lax.rem(me + 1, DEPTH))
    z_dn = remote(x_ref.at[pl.ds(0, 2)], cells.at[pl.ds(Z + 2, 2), body], z_send, z_recv, 1, "depth", lax.rem(me + DEPTH - 1, DEPTH))
    x_up = remote(row_pack.at[1], row_halo.at[0], x_send, x_recv, 0, "ix", lax.rem(ix + 1, n_ix))
    x_dn = remote(row_pack.at[0], row_halo.at[1], x_send, x_recv, 1, "ix", lax.rem(ix + n_ix - 1, n_ix))
    y_up = remote(pack.at[1], halo.at[0], y_send, y_recv, 0, "iy", lax.rem(iy + 1, n_iy))
    y_dn = remote(pack.at[0], halo.at[1], y_send, y_recv, 1, "iy", lax.rem(iy + n_iy - 1, n_iy))

    pl.when(back)(z_up.start)
    pl.when(front)(z_dn.start)

    @pl.when(jnp.logical_not(front))
    def _():
        cells[0:2] = jnp.zeros((2,) + cells.shape[1:], BF16)

    @pl.when(jnp.logical_not(back))
    def _():
        cells[Z + 2 : Z + 4] = jnp.zeros((2,) + cells.shape[1:], BF16)

    for b in range(DEPTH):
        load(b).wait()

    def pack_rows(c, _):
        layers = pl.ds(2 + 8 * c, 8)
        at = pl.ds(pl.multiple_of(16 * c, 16), 16)
        for side, row in ((0, EDGE), (1, X)):
            tiles = cells[layers, row : row + 16].reshape(128, Y)
            row_pack[side, at] = jnp.dot(row_mat[side], tiles, preferred_element_type=F32).astype(BF16)
        return 0

    lax.fori_loop(0, Z // 8, pack_rows, 0)
    pl.when(down)(x_up.start)
    pl.when(up)(x_dn.start)

    def pack_columns(b, _):
        rows = pl.ds(pl.multiple_of(EDGE + ROWS * b, EDGE), ROWS)
        layer_of = (lax.broadcasted_iota(jnp.int32, (ROWS, 256), 1) & 127) >> 1

        def chunk(c, total):
            tiles = cells[pl.ds(2 + 8 * c, 8), rows].reshape(8 * ROWS, Y)
            picked = jnp.dot(tiles, col_mat[...], preferred_element_type=F32).reshape(8, ROWS, 256)
            for i in range(8):
                total = jnp.where(layer_of == 8 * c + i, picked[i], total)
            return total

        total = lax.fori_loop(0, Z // 8, chunk, jnp.zeros((ROWS, 256), F32)).astype(BF16)
        at = pl.ds(pl.multiple_of(ROWS * b, ROWS), ROWS)
        pack[0, at] = total[:, :128]
        pack[1, at] = total[:, 128:]
        return 0

    lax.fori_loop(0, DEPTH, pack_columns, 0)
    pl.when(right)(y_up.start)
    pl.when(left)(y_dn.start)

    for has, copy, buf in ((up, x_up, row_halo.at[0]), (down, x_dn, row_halo.at[1]), (left, y_up, halo.at[0]), (right, y_dn, halo.at[1])):
        pl.when(has)(copy.wait_recv)

        @pl.when(jnp.logical_not(has))
        def _(buf=buf):
            buf[...] = jnp.zeros(buf.shape, BF16)

    pl.when(front)(z_up.wait_recv)
    pl.when(back)(z_dn.wait_recv)

    def unpack_rows(c, _):
        layers = pl.ds(2 + 8 * c, 8)
        at = pl.ds(pl.multiple_of(16 * c, 16), 16)
        for side, row in ((0, 0), (1, X + EDGE)):
            tiles = jnp.dot(unrow_mat[side], row_halo[side, at], preferred_element_type=F32)
            cells[layers, row : row + 16] = tiles.astype(BF16).reshape(8, 16, Y)
        return 0

    lax.fori_loop(0, Z // 8, unpack_rows, 0)

    slots = ((gy0, g0), (gy1, g1))

    def place(n):
        return lax.rem(me + 1 + (n >> 3), DEPTH), n & 7

    def slopes_y(n, slot):
        b, c = place(n)
        rows = pl.ds(pl.multiple_of(ROWS * b, ROWS), ROWS)
        inner = pl.ds(pl.multiple_of(EDGE + ROWS * b, EDGE), ROWS)
        sides = jnp.concatenate([halo[0, rows], halo[1, rows]], axis=1)
        layer_of = (lax.broadcasted_iota(jnp.int32, (ROWS, 256), 1) & 127) >> 1
        outer = jnp.stack([jnp.where(layer_of == 8 * c + i, sides, jnp.zeros_like(sides)) for i in range(8)])
        tiles = cells[pl.ds(2 + 8 * c, 8), inner].reshape(8 * ROWS, Y)
        gy = jnp.dot(tiles, y_mat[:Y], preferred_element_type=F32)
        gy += jnp.dot(outer.reshape(8 * ROWS, 256), y_mat[Y:], preferred_element_type=F32)
        slots[slot][0][...] = gy.reshape(8, ROWS, Y)

    def slopes_zx(n, slot, j):
        b, c = place(n)
        z = 8 * c + 2 * j
        wide = pl.ds(pl.multiple_of(ROWS * b, ROWS), ROWS + 2 * EDGE)
        inner = pl.ds(pl.multiple_of(EDGE + ROWS * b, EDGE), ROWS)
        tiles = [cells[z, inner], cells[z + 1, inner], cells[z + 2, wide], cells[z + 3, wide], cells[z + 4, inner], cells[z + 5, inner]]
        g = jnp.dot(zx_mat[...], jnp.concatenate(tiles, axis=0), preferred_element_type=F32)
        slots[slot][1][:, 2 * j : 2 * j + 2] = g.reshape(3, 2, ROWS, Y)

    def march(n, slot, s):
        b, c = place(n)
        gy_ref, g_ref = slots[slot]
        row, lane = (s // 2) * 16, (s % 2) * 128
        rs, ls = slice(row, row + 16), slice(lane, lane + 128)
        inner = pl.ds(pl.multiple_of(EDGE + ROWS * b + row, EDGE), 16)
        t, w_sum, r_sum, g_sum = (parts[b, k, rs, ls] for k in range(4))
        for i in range(8):
            d = cells[2 + 8 * c + i, inner, ls].astype(F32)
            gx, gz, gy = g_ref[0, i, rs, ls], g_ref[1, i, rs, ls], gy_ref[i, rs, ls]
            s25 = g_ref[2, i, rs, ls] + 16.0 * gy
            n2 = gx * gx + gz * gz + (gy * gy + 144.0)
            bright = jnp.abs(s25) * lax.rsqrt(n2) + BASE
            grow = jnp.exp2(d * EXP2_2D)
            k5 = grow + pltpu.reciprocal(grow, approx=True)
            t_next = t * jnp.exp2(k5 * EXP2_K)
            w = (t - t_next) * bright
            t = t_next
            w_sum = w_sum + w
            r_sum = r_sum + w * jnp.tanh(d)
            g_sum = g_sum + w * jnp.exp2(d * (d * EXP2_SQ))
        for k, v in enumerate((t, w_sum, r_sum, g_sum)):
            parts[b, k, rs, ls] = v

    def send(b):
        return pltpu.make_async_remote_copy(
            src_ref=parts.at[b], dst_ref=got.at[me], send_sem=send_sem.at[b], recv_sem=recv_sem.at[me],
            device_id={"depth": b}, device_id_type=MESH,
        )

    slopes_y(0, 0)
    for j in range(4):
        slopes_zx(0, 0, j)

    def pair(k, _):
        b = lax.rem(me + 1 + (k >> 2), DEPTH)

        @pl.when((k & 3) == 0)
        def _():
            parts[b, 0] = jnp.ones((ROWS, Y), F32)
            for i in (1, 2, 3):
                parts[b, i] = jnp.zeros((ROWS, Y), F32)

        for h in range(2):
            n = 2 * k + h
            slopes_y(n + 1, 1 - h)
            for s in range(4):
                slopes_zx(n + 1, 1 - h, s)
                march(n, h, s)

        @pl.when(jnp.logical_and((k & 3) == 3, k < 4 * DEPTH - 4))
        def _():
            send(b).start()

        return 0

    lax.fori_loop(0, 4 * DEPTH, pair, 0)

    got[me] = parts[me]
    for step in range(1, DEPTH):
        src = lax.rem(me + step, DEPTH)
        pltpu.make_async_remote_copy(
            src_ref=parts.at[src], dst_ref=got.at[src], send_sem=send_sem.at[src], recv_sem=recv_sem.at[src],
            device_id={"depth": src}, device_id_type=MESH,
        ).wait_recv()

    through = got[0, 0]
    w_sum, r_sum, g_sum = got[0, 1], got[0, 2], got[0, 3]
    for i in range(1, DEPTH):
        w_sum += through * got[i, 1]
        r_sum += through * got[i, 2]
        g_sum += through * got[i, 3]
        through = through * got[i, 0]
    out_ref[0] = (w_sum + r_sum) * (0.5 * 0.7 / 25.0)
    out_ref[1] = g_sum * (0.7 / 25.0)
    out_ref[2] = (w_sum - r_sum) * (0.5 * 0.7 / 25.0)
    out_ref[3] = 1.0 - through

    for step in range(1, DEPTH):
        send(lax.rem(me + step, DEPTH)).wait_send()
    for has, copy in ((back, z_up), (front, z_dn), (down, x_up), (up, x_dn), (right, y_up), (left, y_dn)):
        pl.when(has)(copy.wait_send)


def on_device(density):
    rows = pick_rows()
    mats = [jnp.asarray(m, BF16) for m in (along_y(), along_zx(), pick_columns(), rows, rows[::-1].transpose(0, 2, 1))]
    vmem, dma = pl.BlockSpec(memory_space=pltpu.VMEM), pltpu.SemaphoreType.DMA
    return pl.pallas_call(
        kernel,
        out_shape=jax.ShapeDtypeStruct((4, ROWS, Y), F32),
        in_specs=[pl.BlockSpec(memory_space=pl.ANY)] + [vmem] * 5,
        out_specs=vmem,
        scratch_shapes=[
            pltpu.VMEM((Z + 4, X + 2 * EDGE, Y), BF16),
            pltpu.VMEM((2, X, 128), BF16),
            pltpu.VMEM((2, X, 128), BF16),
            pltpu.VMEM((2, 2 * Z, Y), BF16),
            pltpu.VMEM((2, 2 * Z, Y), BF16),
            pltpu.VMEM((DEPTH, 4, ROWS, Y), F32),
            pltpu.VMEM((DEPTH, 4, ROWS, Y), F32),
        ]
        + [pltpu.VMEM((8, ROWS, Y), F32), pltpu.VMEM((3, 8, ROWS, Y), F32)] * 2
        + [dma((DEPTH,))]
        + [dma((2,))] * 6
        + [dma((DEPTH,))] * 2,
        compiler_params=pltpu.CompilerParams(collective_id=0, has_side_effects=True, vmem_limit_bytes=48 << 20),
        name="render",
    )(density, *mats)


def solution(mesh):
    return jax.shard_map(
        on_device,
        mesh=mesh,
        in_specs=(P("depth", "ix", "iy"),),
        out_specs=P(None, ("ix", "depth"), "iy"),
        check_vma=False,
    )
```

```python
import jax
import jax.numpy as jnp
import numpy as np
from jax import lax
from jax.experimental import pallas as pl
from jax.experimental.pallas import tpu as pltpu
from jax.sharding import PartitionSpec as P

MESH = pl.DeviceIdType.MESH
F32, BF16 = jnp.float32, jnp.bfloat16
Z, X, Y = 64, 256, 256
DEPTH = 8
ROWS = X // DEPTH
EDGE = 16
NZ = 512
EXP2_2D = float(2.0 * np.log2(np.e))
EXP2_K = float(-0.1 * np.log2(np.e) / NZ)
EXP2_SQ = float(-np.log2(np.e))
BASE = 25.0 * 0.3 / 0.7


def tap(step):
    near = jnp.where(step == 1, 8.0, jnp.where(step == -1, -8.0, 0.0))
    return jnp.where(step == 2, -1.0, jnp.where(step == -2, 1.0, near))


def fill_matrices(y_mat, zx_mat, pick, spread):
    k, y = (lax.broadcasted_iota(jnp.int32, (256, Y), i) for i in (0, 1))
    y_mat[:256] = tap(k - y).astype(BF16)
    y_mat[256:] = tap(jnp.where(k < 128, (k & 1) - 2, Y + (k & 1)) - y).astype(BF16)
    m, c = (lax.broadcasted_iota(jnp.int32, (2 * ROWS, 256), i) for i in (0, 1))
    layer, row = m >> 5, m & 31
    at = jnp.where(c < 64, c >> 5, jnp.where(c < 192, 1 + (c >> 6), (c >> 5) - 2))
    across = jnp.where((c >= 64) & (c < 192), (c & 63) - EDGE, c & 31)
    gx = jnp.where(at == layer + 2, tap(across - row), 0.0)
    gz = jnp.where(across == row, tap(at - 2 - layer), 0.0)
    for i, g in enumerate((gx, gz, 15.0 * gx + 12.0 * gz)):
        zx_mat[2 * ROWS * i : 2 * ROWS * (i + 1)] = g.astype(BF16)
    m, c = (lax.broadcasted_iota(jnp.int32, (16, 128), i) for i in (0, 1))
    o, q = (lax.broadcasted_iota(jnp.int32, (128, 16), i) for i in (0, 1))
    for side, start in ((0, 0), (1, 14)):
        pick[side] = jnp.where(((c >> 4) == (m >> 1)) & ((c & 15) == start + (m & 1)), 1.0, 0.0).astype(BF16)
        spread[1 - side] = jnp.where(((o >> 4) == (q >> 1)) & ((o & 15) == start + (q & 1)), 1.0, 0.0).astype(BF16)


def kernel(
    x_ref, out_ref,
    y_mat, zx_mat, pick, spread, cells, halo, pack, row_pack, row_halo, parts, got, gy0, g0, gy1, g1,
    load_sem, z_send, z_recv, x_send, x_recv, y_send, y_recv, send_sem, recv_sem,
):
    me = lax.axis_index("depth")
    ix, iy = lax.axis_index("ix"), lax.axis_index("iy")
    n_ix, n_iy = lax.axis_size("ix"), lax.axis_size("iy")
    front, back = me > 0, me < DEPTH - 1
    up, down = ix > 0, ix < n_ix - 1
    left, right = iy > 0, iy < n_iy - 1

    def load(b):
        rows = pl.ds(pl.multiple_of(ROWS * b, ROWS), ROWS)
        inner = pl.ds(pl.multiple_of(EDGE + ROWS * b, EDGE), ROWS)
        return pltpu.make_async_copy(x_ref.at[:, rows], cells.at[pl.ds(2, Z), inner], load_sem.at[b])

    for i in range(DEPTH):
        load(lax.rem(me + 1 + i, DEPTH)).start()

    barrier = pltpu.get_barrier_semaphore()
    for step in range(1, DEPTH):
        pl.semaphore_signal(barrier, inc=1, device_id={"depth": lax.rem(me + step, DEPTH)}, device_id_type=MESH)
    for axis, at, count in (("ix", ix, n_ix), ("iy", iy, n_iy)):
        for step in (1, count - 1):
            pl.semaphore_signal(barrier, inc=1, device_id={axis: lax.rem(at + step, count)}, device_id_type=MESH)
    pl.semaphore_wait(barrier, DEPTH - 1 + 4)

    def remote(src, dst, sems, recvs, k, axis, to):
        return pltpu.make_async_remote_copy(
            src_ref=src, dst_ref=dst, send_sem=sems.at[k], recv_sem=recvs.at[k],
            device_id={axis: to}, device_id_type=MESH,
        )

    body = pl.ds(EDGE, X)
    z_up = remote(x_ref.at[pl.ds(Z - 2, 2)], cells.at[pl.ds(0, 2), body], z_send, z_recv, 0, "depth", lax.rem(me + 1, DEPTH))
    z_dn = remote(x_ref.at[pl.ds(0, 2)], cells.at[pl.ds(Z + 2, 2), body], z_send, z_recv, 1, "depth", lax.rem(me + DEPTH - 1, DEPTH))
    x_up = remote(row_pack.at[1], row_halo.at[0], x_send, x_recv, 0, "ix", lax.rem(ix + 1, n_ix))
    x_dn = remote(row_pack.at[0], row_halo.at[1], x_send, x_recv, 1, "ix", lax.rem(ix + n_ix - 1, n_ix))

    def y_copies(b):
        low = pltpu.make_async_remote_copy(
            src_ref=pack.at[1, b], dst_ref=halo.at[0, b], send_sem=y_send.at[0, b], recv_sem=y_recv.at[0, b],
            device_id={"iy": lax.rem(iy + 1, n_iy)}, device_id_type=MESH,
        )
        high = pltpu.make_async_remote_copy(
            src_ref=pack.at[0, b], dst_ref=halo.at[1, b], send_sem=y_send.at[1, b], recv_sem=y_recv.at[1, b],
            device_id={"iy": lax.rem(iy + n_iy - 1, n_iy)}, device_id_type=MESH,
        )
        return low, high

    pl.when(back)(z_up.start)
    pl.when(front)(z_dn.start)

    @pl.when(jnp.logical_not(front))
    def _():
        cells[0:2] = jnp.zeros((2,) + cells.shape[1:], BF16)

    @pl.when(jnp.logical_not(back))
    def _():
        cells[Z + 2 : Z + 4] = jnp.zeros((2,) + cells.shape[1:], BF16)


    fill_matrices(y_mat, zx_mat, pick, spread)
    for side, has in ((0, left), (1, right)):

        @pl.when(jnp.logical_not(has))
        def _(side=side):
            halo[side] = jnp.zeros(halo.shape[1:], BF16)

    for side, has in ((0, up), (1, down)):

        @pl.when(jnp.logical_not(has))
        def _(side=side):
            row_halo[side] = jnp.zeros(row_halo.shape[1:], BF16)

    lane = lax.broadcasted_iota(jnp.int32, (16, 128), 1)

    def pack_columns(b, half):
        rows = pl.ds(pl.multiple_of(EDGE + ROWS * b + 16 * half, EDGE), 16)
        first, last = jnp.zeros((16, 128), F32), jnp.zeros((16, 128), F32)
        for z in range(Z):
            ends = jnp.where(lane < 2, cells[2 + z, rows, :128].astype(F32), cells[2 + z, rows, Y - 128 :].astype(F32))
            moved = pltpu.roll(ends, 2 * z, axis=1) if z else ends
            first = jnp.where(lane >> 1 == z, moved, first)
            last = jnp.where(lane >> 1 == (z + 63) & 63, moved, last)
        last = pltpu.roll(last, 2, axis=1)
        at = pl.ds(pl.multiple_of(16 * half, 16), 16)
        pack[0, b, at] = first.astype(BF16)
        pack[1, b, at] = last.astype(BF16)

    def pack_block(i, _):
        b = lax.rem(me + 1 + i, DEPTH)
        load(b).wait()

        def one(half, _):
            pack_columns(b, half)
            return 0

        lax.fori_loop(0, 2, one, 0)
        low, high = y_copies(b)
        pl.when(right)(low.start)
        pl.when(left)(high.start)
        return 0

    pack_block(0, 0)
    lax.fori_loop(1, DEPTH, pack_block, 0)
    for side, row in ((0, EDGE), (1, X)):
        for c in range(Z // 8):
            tiles = cells[2 + 8 * c : 10 + 8 * c, row : row + 16].reshape(128, Y)
            picked = jnp.dot(pick[side], tiles, preferred_element_type=F32)
            row_pack[side, 16 * c : 16 * c + 16] = picked.astype(BF16)
    pl.when(down)(x_up.start)
    pl.when(up)(x_dn.start)

    pl.when(front)(z_up.wait_recv)
    pl.when(back)(z_dn.wait_recv)
    pl.when(up)(x_up.wait_recv)
    pl.when(down)(x_dn.wait_recv)
    for side, row in ((0, 0), (1, X + EDGE)):
        for c in range(Z // 8):
            tiles = jnp.dot(spread[side], row_halo[side, 16 * c : 16 * c + 16], preferred_element_type=F32)
            cells[2 + 8 * c : 10 + 8 * c, row : row + 16] = tiles.astype(BF16).reshape(8, 16, Y)

    def wait_sides(b):
        low, high = y_copies(b)
        pl.when(left)(low.wait_recv)
        pl.when(right)(high.wait_recv)

    wait_sides(lax.rem(me + 1, DEPTH))

    slots = ((gy0, g0), (gy1, g1))

    def place(n):
        return lax.rem(me + 1 + (n >> 3), DEPTH), n & 7

    def slopes_y(n, slot):
        b, c = place(n)
        inner = pl.ds(pl.multiple_of(EDGE + ROWS * b, EDGE), ROWS)
        sides = jnp.concatenate([halo[0, b], halo[1, b]], axis=1)
        layer_of = (lax.broadcasted_iota(jnp.int32, (ROWS, 256), 1) & 127) >> 1
        outer = jnp.stack([jnp.where(layer_of == 8 * c + i, sides, jnp.zeros_like(sides)) for i in range(8)])
        tiles = cells[pl.ds(2 + 8 * c, 8), inner].reshape(8 * ROWS, Y)
        gy = jnp.dot(tiles, y_mat[:Y], preferred_element_type=F32)
        gy += jnp.dot(outer.reshape(8 * ROWS, 256), y_mat[Y:], preferred_element_type=F32)
        slots[slot][0][...] = gy.reshape(8, ROWS, Y)

    def slopes_zx(n, slot, j):
        b, c = place(n)
        z = 8 * c + 2 * j
        wide = pl.ds(pl.multiple_of(ROWS * b, ROWS), ROWS + 2 * EDGE)
        inner = pl.ds(pl.multiple_of(EDGE + ROWS * b, EDGE), ROWS)
        tiles = [cells[z, inner], cells[z + 1, inner], cells[z + 2, wide], cells[z + 3, wide], cells[z + 4, inner], cells[z + 5, inner]]
        g = jnp.dot(zx_mat[...], jnp.concatenate(tiles, axis=0), preferred_element_type=F32)
        slots[slot][1][:, 2 * j : 2 * j + 2] = g.reshape(3, 2, ROWS, Y)

    def march(n, slot, s):
        b, c = place(n)
        gy_ref, g_ref = slots[slot]
        row, lane = (s // 2) * 16, (s % 2) * 128
        rs, ls = slice(row, row + 16), slice(lane, lane + 128)
        inner = pl.ds(pl.multiple_of(EDGE + ROWS * b + row, EDGE), 16)
        t, w_sum, r_sum, g_sum = (parts[b, k, rs, ls] for k in range(4))
        for i in range(8):
            d = cells[2 + 8 * c + i, inner, ls].astype(F32)
            gx, gz, gy = g_ref[0, i, rs, ls], g_ref[1, i, rs, ls], gy_ref[i, rs, ls]
            s25 = g_ref[2, i, rs, ls] + 16.0 * gy
            n2 = gx * gx + gz * gz + (gy * gy + 144.0)
            bright = jnp.abs(s25) * lax.rsqrt(n2) + BASE
            grow = jnp.exp2(d * EXP2_2D)
            k5 = grow + pltpu.reciprocal(grow, approx=True)
            t_next = t * jnp.exp2(k5 * EXP2_K)
            w = (t - t_next) * bright
            t = t_next
            w_sum = w_sum + w
            r_sum = r_sum + w * jnp.tanh(d)
            g_sum = g_sum + w * jnp.exp2(d * (d * EXP2_SQ))
        for k, v in enumerate((t, w_sum, r_sum, g_sum)):
            parts[b, k, rs, ls] = v

    def send(b):
        return pltpu.make_async_remote_copy(
            src_ref=parts.at[b], dst_ref=got.at[me], send_sem=send_sem.at[b], recv_sem=recv_sem.at[me],
            device_id={"depth": b}, device_id_type=MESH,
        )

    slopes_y(0, 0)
    for j in range(4):
        slopes_zx(0, 0, j)

    def pair(k, _):
        b = lax.rem(me + 1 + (k >> 2), DEPTH)

        @pl.when((k & 3) == 0)
        def _():
            parts[b, 0] = jnp.ones((ROWS, Y), F32)
            for i in (1, 2, 3):
                parts[b, i] = jnp.zeros((ROWS, Y), F32)

        @pl.when(jnp.logical_and((k & 3) == 3, k < 4 * DEPTH - 1))
        def _():
            wait_sides(lax.rem(b + 1, DEPTH))

        for h in range(2):
            n = 2 * k + h
            slopes_y(n + 1, 1 - h)
            for s in range(4):
                slopes_zx(n + 1, 1 - h, s)
                march(n, h, s)

        @pl.when(jnp.logical_and((k & 3) == 3, k < 4 * DEPTH - 4))
        def _():
            send(b).start()

        return 0

    lax.fori_loop(0, 4 * DEPTH, pair, 0)

    got[me] = parts[me]
    for step in range(1, DEPTH):
        src = lax.rem(me + step, DEPTH)
        pltpu.make_async_remote_copy(
            src_ref=parts.at[src], dst_ref=got.at[src], send_sem=send_sem.at[src], recv_sem=recv_sem.at[src],
            device_id={"depth": src}, device_id_type=MESH,
        ).wait_recv()

    through = got[0, 0]
    w_sum, r_sum, g_sum = got[0, 1], got[0, 2], got[0, 3]
    for i in range(1, DEPTH):
        w_sum += through * got[i, 1]
        r_sum += through * got[i, 2]
        g_sum += through * got[i, 3]
        through = through * got[i, 0]
    out_ref[0] = (w_sum + r_sum) * (0.5 * 0.7 / 25.0)
    out_ref[1] = g_sum * (0.7 / 25.0)
    out_ref[2] = (w_sum - r_sum) * (0.5 * 0.7 / 25.0)
    out_ref[3] = 1.0 - through

    for step in range(1, DEPTH):
        send(lax.rem(me + step, DEPTH)).wait_send()
    for has, copy in ((back, z_up), (front, z_dn), (down, x_up), (up, x_dn)):
        pl.when(has)(copy.wait_send)
    for b in range(DEPTH):
        low, high = y_copies(b)
        pl.when(right)(low.wait_send)
        pl.when(left)(high.wait_send)


def on_device(density):
    vmem, dma = pl.BlockSpec(memory_space=pltpu.VMEM), pltpu.SemaphoreType.DMA
    return pl.pallas_call(
        kernel,
        out_shape=jax.ShapeDtypeStruct((4, ROWS, Y), F32),
        in_specs=[pl.BlockSpec(memory_space=pl.ANY)],
        out_specs=vmem,
        scratch_shapes=[
            pltpu.VMEM((Y + 256, Y), BF16),
            pltpu.VMEM((6 * ROWS, 256), BF16),
            pltpu.VMEM((2, 16, 128), BF16),
            pltpu.VMEM((2, 128, 16), BF16),
            pltpu.VMEM((Z + 4, X + 2 * EDGE, Y), BF16),
            pltpu.VMEM((2, DEPTH, ROWS, 128), BF16),
            pltpu.VMEM((2, DEPTH, ROWS, 128), BF16),
            pltpu.VMEM((2, 2 * Z, Y), BF16),
            pltpu.VMEM((2, 2 * Z, Y), BF16),
            pltpu.VMEM((DEPTH, 4, ROWS, Y), F32),
            pltpu.VMEM((DEPTH, 4, ROWS, Y), F32),
        ]
        + [pltpu.VMEM((8, ROWS, Y), F32), pltpu.VMEM((3, 8, ROWS, Y), F32)] * 2
        + [dma((DEPTH,))]
        + [dma((2,))] * 4
        + [dma((2, DEPTH))] * 2
        + [dma((DEPTH,))] * 2,
        compiler_params=pltpu.CompilerParams(collective_id=0, has_side_effects=True, vmem_limit_bytes=58 << 20),
        name="render",
    )(density)


def solution(mesh):
    return jax.shard_map(
        on_device,
        mesh=mesh,
        in_specs=(P("depth", "ix", "iy"),),
        out_specs=P(None, ("ix", "depth"), "iy"),
        check_vma=False,
    )
```

```python
import jax
import jax.numpy as jnp
import numpy as np
from jax import lax
from jax.experimental import pallas as pl
from jax.experimental.pallas import tpu as pltpu
from jax.sharding import PartitionSpec as P

MESH = pl.DeviceIdType.MESH
F32, BF16 = jnp.float32, jnp.bfloat16
Z, X, Y = 64, 256, 256
DEPTH = 8
ROWS = X // DEPTH
EDGE = 16
NZ = 512
EXP2_2D = float(2.0 * np.log2(np.e))
EXP2_K = float(-0.1 * np.log2(np.e) / NZ)
EXP2_SQ = float(-np.log2(np.e))
BASE = 25.0 * 0.3 / 0.7


def tap(step):
    near = jnp.where(step == 1, 8.0, jnp.where(step == -1, -8.0, 0.0))
    return jnp.where(step == 2, -1.0, jnp.where(step == -2, 1.0, near))


def fill_matrices(y_mat, zx_mat, pick, spread):
    k, y = (lax.broadcasted_iota(jnp.int32, (256, Y), i) for i in (0, 1))
    y_mat[:256] = tap(k - y).astype(BF16)
    y_mat[256:] = tap(jnp.where(k < 128, (k & 1) - 2, Y + (k & 1)) - y).astype(BF16)
    m, c = (lax.broadcasted_iota(jnp.int32, (2 * ROWS, 256), i) for i in (0, 1))
    layer, row = m >> 5, m & 31
    at = jnp.where(c < 64, c >> 5, jnp.where(c < 192, 1 + (c >> 6), (c >> 5) - 2))
    across = jnp.where((c >= 64) & (c < 192), (c & 63) - EDGE, c & 31)
    gx = jnp.where(at == layer + 2, tap(across - row), 0.0)
    gz = jnp.where(across == row, tap(at - 2 - layer), 0.0)
    for i, g in enumerate((gx, gz, 15.0 * gx + 12.0 * gz)):
        zx_mat[2 * ROWS * i : 2 * ROWS * (i + 1)] = g.astype(BF16)
    m, c = (lax.broadcasted_iota(jnp.int32, (16, 128), i) for i in (0, 1))
    o, q = (lax.broadcasted_iota(jnp.int32, (128, 16), i) for i in (0, 1))
    for side, start in ((0, 0), (1, 14)):
        pick[side] = jnp.where(((c >> 4) == (m >> 1)) & ((c & 15) == start + (m & 1)), 1.0, 0.0).astype(BF16)
        spread[1 - side] = jnp.where(((o >> 4) == (q >> 1)) & ((o & 15) == start + (q & 1)), 1.0, 0.0).astype(BF16)


def kernel(
    x_ref, out_ref,
    y_mat, zx_mat, pick, spread, cells, halo, pack, row_pack, row_halo, parts, got,
    load_sem, z_send, z_recv, x_send, x_recv, y_send, y_recv, send_sem, recv_sem, *slopes,
):
    me = lax.axis_index("depth")
    ix, iy = lax.axis_index("ix"), lax.axis_index("iy")
    n_ix, n_iy = lax.axis_size("ix"), lax.axis_size("iy")
    front, back = me > 0, me < DEPTH - 1
    up, down = ix > 0, ix < n_ix - 1
    left, right = iy > 0, iy < n_iy - 1

    def load(b):
        rows = pl.ds(pl.multiple_of(ROWS * b, ROWS), ROWS)
        inner = pl.ds(pl.multiple_of(EDGE + ROWS * b, EDGE), ROWS)
        return pltpu.make_async_copy(x_ref.at[:, rows], cells.at[pl.ds(2, Z), inner], load_sem.at[b])

    for i in range(DEPTH):
        load(lax.rem(me + 1 + i, DEPTH)).start()

    barrier = pltpu.get_barrier_semaphore()
    for step in range(1, DEPTH):
        pl.semaphore_signal(barrier, inc=1, device_id={"depth": lax.rem(me + step, DEPTH)}, device_id_type=MESH)
    for axis, at, count in (("ix", ix, n_ix), ("iy", iy, n_iy)):
        for step in (1, count - 1):
            pl.semaphore_signal(barrier, inc=1, device_id={axis: lax.rem(at + step, count)}, device_id_type=MESH)
    pl.semaphore_wait(barrier, DEPTH - 1 + 4)

    def remote(src, dst, sems, recvs, k, axis, to):
        return pltpu.make_async_remote_copy(
            src_ref=src, dst_ref=dst, send_sem=sems.at[k], recv_sem=recvs.at[k],
            device_id={axis: to}, device_id_type=MESH,
        )

    body = pl.ds(EDGE, X)
    z_up = remote(x_ref.at[pl.ds(Z - 2, 2)], cells.at[pl.ds(0, 2), body], z_send, z_recv, 0, "depth", lax.rem(me + 1, DEPTH))
    z_dn = remote(x_ref.at[pl.ds(0, 2)], cells.at[pl.ds(Z + 2, 2), body], z_send, z_recv, 1, "depth", lax.rem(me + DEPTH - 1, DEPTH))
    x_up = remote(row_pack.at[1], row_halo.at[0], x_send, x_recv, 0, "ix", lax.rem(ix + 1, n_ix))
    x_dn = remote(row_pack.at[0], row_halo.at[1], x_send, x_recv, 1, "ix", lax.rem(ix + n_ix - 1, n_ix))

    def y_copies(b):
        low = pltpu.make_async_remote_copy(
            src_ref=pack.at[1, b], dst_ref=halo.at[0, b], send_sem=y_send.at[0, b], recv_sem=y_recv.at[0, b],
            device_id={"iy": lax.rem(iy + 1, n_iy)}, device_id_type=MESH,
        )
        high = pltpu.make_async_remote_copy(
            src_ref=pack.at[0, b], dst_ref=halo.at[1, b], send_sem=y_send.at[1, b], recv_sem=y_recv.at[1, b],
            device_id={"iy": lax.rem(iy + n_iy - 1, n_iy)}, device_id_type=MESH,
        )
        return low, high

    pl.when(back)(z_up.start)
    pl.when(front)(z_dn.start)

    @pl.when(jnp.logical_not(front))
    def _():
        cells[0:2] = jnp.zeros((2,) + cells.shape[1:], BF16)

    @pl.when(jnp.logical_not(back))
    def _():
        cells[Z + 2 : Z + 4] = jnp.zeros((2,) + cells.shape[1:], BF16)


    fill_matrices(y_mat, zx_mat, pick, spread)
    for side, has in ((0, left), (1, right)):

        @pl.when(jnp.logical_not(has))
        def _(side=side):
            halo[side] = jnp.zeros(halo.shape[1:], BF16)

    for side, has in ((0, up), (1, down)):

        @pl.when(jnp.logical_not(has))
        def _(side=side):
            row_halo[side] = jnp.zeros(row_halo.shape[1:], BF16)

    lane = lax.broadcasted_iota(jnp.int32, (16, 128), 1)

    def pack_columns(b, half):
        rows = pl.ds(pl.multiple_of(EDGE + ROWS * b + 16 * half, EDGE), 16)
        first, last = jnp.zeros((16, 128), F32), jnp.zeros((16, 128), F32)
        for z in range(Z):
            ends = jnp.where(lane < 2, cells[2 + z, rows, :128].astype(F32), cells[2 + z, rows, Y - 128 :].astype(F32))
            moved = pltpu.roll(ends, 2 * z, axis=1) if z else ends
            first = jnp.where(lane >> 1 == z, moved, first)
            last = jnp.where(lane >> 1 == (z + 63) & 63, moved, last)
        last = pltpu.roll(last, 2, axis=1)
        at = pl.ds(pl.multiple_of(16 * half, 16), 16)
        pack[0, b, at] = first.astype(BF16)
        pack[1, b, at] = last.astype(BF16)

    def pack_block(i, _):
        b = lax.rem(me + 1 + i, DEPTH)
        load(b).wait()

        def one(half, _):
            pack_columns(b, half)
            return 0

        lax.fori_loop(0, 2, one, 0)
        low, high = y_copies(b)
        pl.when(right)(low.start)
        pl.when(left)(high.start)
        return 0

    pack_block(0, 0)
    lax.fori_loop(1, DEPTH, pack_block, 0)
    for side, row in ((0, EDGE), (1, X)):
        for c in range(Z // 8):
            tiles = cells[2 + 8 * c : 10 + 8 * c, row : row + 16].reshape(128, Y)
            picked = jnp.dot(pick[side], tiles, preferred_element_type=F32)
            row_pack[side, 16 * c : 16 * c + 16] = picked.astype(BF16)
    pl.when(down)(x_up.start)
    pl.when(up)(x_dn.start)

    pl.when(front)(z_up.wait_recv)
    pl.when(back)(z_dn.wait_recv)
    pl.when(up)(x_up.wait_recv)
    pl.when(down)(x_dn.wait_recv)
    for side, row in ((0, 0), (1, X + EDGE)):
        for c in range(Z // 8):
            tiles = jnp.dot(spread[side], row_halo[side, 16 * c : 16 * c + 16], preferred_element_type=F32)
            cells[2 + 8 * c : 10 + 8 * c, row : row + 16] = tiles.astype(BF16).reshape(8, 16, Y)

    def wait_sides(b):
        low, high = y_copies(b)
        pl.when(left)(low.wait_recv)
        pl.when(right)(high.wait_recv)

    wait_sides(lax.rem(me + 1, DEPTH))

    slots = tuple(zip(slopes[:4], slopes[4:]))

    def place(n):
        return lax.rem(me + 1 + (n >> 3), DEPTH), n & 7

    def slopes_y(n, first):
        b, c = place(n)
        inner = pl.ds(pl.multiple_of(EDGE + ROWS * b, EDGE), ROWS)
        sides = jnp.concatenate([halo[0, b], halo[1, b]], axis=1)
        layer_of = (lax.broadcasted_iota(jnp.int32, (ROWS, 256), 1) & 127) >> 1
        outer = jnp.stack([jnp.where(layer_of == 8 * c + i, sides, jnp.zeros_like(sides)) for i in range(16)])
        tiles = cells[pl.ds(2 + 8 * c, 16), inner].reshape(16 * ROWS, Y)
        gy = jnp.dot(tiles, y_mat[:Y], preferred_element_type=F32)
        gy += jnp.dot(outer.reshape(16 * ROWS, 256), y_mat[Y:], preferred_element_type=F32)
        gy = gy.reshape(2, 8, ROWS, Y)
        slots[first][0][...] = gy[0]
        slots[first + 1][0][...] = gy[1]

    def slopes_zx(n, slot, j):
        b, c = place(n)
        z = 8 * c + 2 * j
        wide = pl.ds(pl.multiple_of(ROWS * b, ROWS), ROWS + 2 * EDGE)
        inner = pl.ds(pl.multiple_of(EDGE + ROWS * b, EDGE), ROWS)
        tiles = [cells[z, inner], cells[z + 1, inner], cells[z + 2, wide], cells[z + 3, wide], cells[z + 4, inner], cells[z + 5, inner]]
        g = jnp.dot(zx_mat[...], jnp.concatenate(tiles, axis=0), preferred_element_type=F32)
        slots[slot][1][:, 2 * j : 2 * j + 2] = g.reshape(3, 2, ROWS, Y)

    def march(n, slot, s):
        b, c = place(n)
        gy_ref, g_ref = slots[slot]
        row, lane = (s // 2) * 16, (s % 2) * 128
        rs, ls = slice(row, row + 16), slice(lane, lane + 128)
        inner = pl.ds(pl.multiple_of(EDGE + ROWS * b + row, EDGE), 16)
        t, w_sum, r_sum, g_sum = (parts[b, k, rs, ls] for k in range(4))
        for i in range(8):
            d = cells[2 + 8 * c + i, inner, ls].astype(F32)
            gx, gz, gy = g_ref[0, i, rs, ls], g_ref[1, i, rs, ls], gy_ref[i, rs, ls]
            s25 = g_ref[2, i, rs, ls] + 16.0 * gy
            n2 = gx * gx + gz * gz + (gy * gy + 144.0)
            bright = jnp.abs(s25) * lax.rsqrt(n2) + BASE
            grow = jnp.exp2(d * EXP2_2D)
            k5 = grow + pltpu.reciprocal(grow, approx=True)
            t_next = t * jnp.exp2(k5 * EXP2_K)
            w = (t - t_next) * bright
            t = t_next
            w_sum = w_sum + w
            r_sum = r_sum + w * jnp.tanh(d)
            g_sum = g_sum + w * jnp.exp2(d * (d * EXP2_SQ))
        for k, v in enumerate((t, w_sum, r_sum, g_sum)):
            parts[b, k, rs, ls] = v

    def send(b):
        return pltpu.make_async_remote_copy(
            src_ref=parts.at[b], dst_ref=got.at[me], send_sem=send_sem.at[b], recv_sem=recv_sem.at[me],
            device_id={"depth": b}, device_id_type=MESH,
        )

    slopes_y(0, 0)
    for q in range(2):
        for j in range(4):
            slopes_zx(q, q, j)

    def half_block(k, _):
        b = lax.rem(me + 1 + (k >> 1), DEPTH)

        @pl.when((k & 1) == 0)
        def _():
            parts[b, 0] = jnp.ones((ROWS, Y), F32)
            for i in (1, 2, 3):
                parts[b, i] = jnp.zeros((ROWS, Y), F32)

        @pl.when(jnp.logical_and((k & 1) == 1, k < 2 * DEPTH - 1))
        def _():
            wait_sides(lax.rem(b + 1, DEPTH))

        for h in range(2):
            @pl.when(k + me >= 0)
            def _(h=h):
                n = 4 * k + 2 * h
                use, fill = 2 * h, 2 - 2 * h
                slopes_y(n + 2, fill)
                for i in range(8):
                    slopes_zx(n + 2 + i // 4, fill + i // 4, i % 4)
                    march(n + i % 2, use + i % 2, i // 2)

        @pl.when(jnp.logical_and((k & 1) == 1, k < 2 * DEPTH - 2))
        def _():
            send(b).start()

        return 0

    lax.fori_loop(0, 2 * DEPTH, half_block, 0)

    got[me] = parts[me]
    for step in range(1, DEPTH):
        src = lax.rem(me + step, DEPTH)
        pltpu.make_async_remote_copy(
            src_ref=parts.at[src], dst_ref=got.at[src], send_sem=send_sem.at[src], recv_sem=recv_sem.at[src],
            device_id={"depth": src}, device_id_type=MESH,
        ).wait_recv()

    through = got[0, 0]
    w_sum, r_sum, g_sum = got[0, 1], got[0, 2], got[0, 3]
    for i in range(1, DEPTH):
        w_sum += through * got[i, 1]
        r_sum += through * got[i, 2]
        g_sum += through * got[i, 3]
        through = through * got[i, 0]
    out_ref[0] = (w_sum + r_sum) * (0.5 * 0.7 / 25.0)
    out_ref[1] = g_sum * (0.7 / 25.0)
    out_ref[2] = (w_sum - r_sum) * (0.5 * 0.7 / 25.0)
    out_ref[3] = 1.0 - through

    for step in range(1, DEPTH):
        send(lax.rem(me + step, DEPTH)).wait_send()
    for has, copy in ((back, z_up), (front, z_dn), (down, x_up), (up, x_dn)):
        pl.when(has)(copy.wait_send)
    for b in range(DEPTH):
        low, high = y_copies(b)
        pl.when(right)(low.wait_send)
        pl.when(left)(high.wait_send)


def on_device(density):
    vmem, dma = pl.BlockSpec(memory_space=pltpu.VMEM), pltpu.SemaphoreType.DMA
    return pl.pallas_call(
        kernel,
        out_shape=jax.ShapeDtypeStruct((4, ROWS, Y), F32),
        in_specs=[pl.BlockSpec(memory_space=pl.ANY)],
        out_specs=vmem,
        scratch_shapes=[
            pltpu.VMEM((Y + 256, Y), BF16),
            pltpu.VMEM((6 * ROWS, 256), BF16),
            pltpu.VMEM((2, 16, 128), BF16),
            pltpu.VMEM((2, 128, 16), BF16),
            pltpu.VMEM((Z + 4, X + 2 * EDGE, Y), BF16),
            pltpu.VMEM((2, DEPTH, ROWS, 128), BF16),
            pltpu.VMEM((2, DEPTH, ROWS, 128), BF16),
            pltpu.VMEM((2, 2 * Z, Y), BF16),
            pltpu.VMEM((2, 2 * Z, Y), BF16),
            pltpu.VMEM((DEPTH, 4, ROWS, Y), F32),
            pltpu.VMEM((DEPTH, 4, ROWS, Y), F32),
        ]
        + [dma((DEPTH,))]
        + [dma((2,))] * 4
        + [dma((2, DEPTH))] * 2
        + [dma((DEPTH,))] * 2
        + [pltpu.VMEM((8, ROWS, Y), F32)] * 4
        + [pltpu.VMEM((3, 8, ROWS, Y), F32)] * 4,
        compiler_params=pltpu.CompilerParams(collective_id=0, has_side_effects=True, vmem_limit_bytes=48 << 20),
        name="render",
    )(density)


def solution(mesh):
    return jax.shard_map(
        on_device,
        mesh=mesh,
        in_specs=(P("depth", "ix", "iy"),),
        out_specs=P(None, ("ix", "depth"), "iy"),
        check_vma=False,
    )
```

```python
import jax
import jax.numpy as jnp
import numpy as np
from jax import lax
from jax.experimental import pallas as pl
from jax.experimental.pallas import tpu as pltpu
from jax.sharding import PartitionSpec as P

MESH = pl.DeviceIdType.MESH
F32, BF16 = jnp.float32, jnp.bfloat16
Z, X, Y = 64, 256, 256
DEPTH = 8
ROWS = X // DEPTH
EDGE = 16
NZ = 512
EXP2_2D = float(2.0 * np.log2(np.e))
EXP2_K = float(-0.1 * np.log2(np.e) / NZ)
EXP2_SQ = float(-np.log2(np.e))
BASE = 25.0 * 0.3 / 0.7


def tap(step):
    near = jnp.where(step == 1, 8.0, jnp.where(step == -1, -8.0, 0.0))
    return jnp.where(step == 2, -1.0, jnp.where(step == -2, 1.0, near))


def fill_matrices(y_mat, zx_mat, pick, spread):
    k, y = (lax.broadcasted_iota(jnp.int32, (256, Y), i) for i in (0, 1))
    y_mat[:256] = tap(k - y).astype(BF16)
    y_mat[256:] = tap(jnp.where(k < 128, (k & 1) - 2, Y + (k & 1)) - y).astype(BF16)
    m, c = (lax.broadcasted_iota(jnp.int32, (2 * ROWS, 256), i) for i in (0, 1))
    layer, row = m >> 5, m & 31
    at = jnp.where(c < 64, c >> 5, jnp.where(c < 192, 1 + (c >> 6), (c >> 5) - 2))
    across = jnp.where((c >= 64) & (c < 192), (c & 63) - EDGE, c & 31)
    gx = jnp.where(at == layer + 2, tap(across - row), 0.0)
    gz = jnp.where(across == row, tap(at - 2 - layer), 0.0)
    for i, g in enumerate((gx, gz, 15.0 * gx + 12.0 * gz)):
        zx_mat[2 * ROWS * i : 2 * ROWS * (i + 1)] = g.astype(BF16)
    m, c = (lax.broadcasted_iota(jnp.int32, (16, 128), i) for i in (0, 1))
    o, q = (lax.broadcasted_iota(jnp.int32, (128, 16), i) for i in (0, 1))
    for side, start in ((0, 0), (1, 14)):
        pick[side] = jnp.where(((c >> 4) == (m >> 1)) & ((c & 15) == start + (m & 1)), 1.0, 0.0).astype(BF16)
        spread[1 - side] = jnp.where(((o >> 4) == (q >> 1)) & ((o & 15) == start + (q & 1)), 1.0, 0.0).astype(BF16)


def kernel(
    x_ref, out_ref,
    y_mat, zx_mat, pick, spread, cells, halo, pack, row_pack, row_halo, parts, got,
    load_sem, z_send, z_recv, x_send, x_recv, y_send, y_recv, send_sem, recv_sem, *slopes,
):
    me = lax.axis_index("depth")
    ix, iy = lax.axis_index("ix"), lax.axis_index("iy")
    n_ix, n_iy = lax.axis_size("ix"), lax.axis_size("iy")
    front, back = me > 0, me < DEPTH - 1
    up, down = ix > 0, ix < n_ix - 1
    left, right = iy > 0, iy < n_iy - 1

    def load(b):
        rows = pl.ds(pl.multiple_of(ROWS * b, ROWS), ROWS)
        inner = pl.ds(pl.multiple_of(EDGE + ROWS * b, EDGE), ROWS)
        return pltpu.make_async_copy(x_ref.at[:, rows], cells.at[pl.ds(2, Z), inner], load_sem.at[b])

    barrier = pltpu.get_barrier_semaphore()
    for step in range(1, DEPTH):
        pl.semaphore_signal(barrier, inc=1, device_id={"depth": lax.rem(me + step, DEPTH)}, device_id_type=MESH)
    for axis, at, count in (("ix", ix, n_ix), ("iy", iy, n_iy)):
        for step in (1, count - 1):
            pl.semaphore_signal(barrier, inc=1, device_id={axis: lax.rem(at + step, count)}, device_id_type=MESH)
    for i in range(DEPTH):
        load(lax.rem(me + 1 + i, DEPTH)).start()

    def remote(src, dst, sems, recvs, k, axis, to):
        return pltpu.make_async_remote_copy(
            src_ref=src, dst_ref=dst, send_sem=sems.at[k], recv_sem=recvs.at[k],
            device_id={axis: to}, device_id_type=MESH,
        )

    def z_copies(b):
        rows = pl.ds(pl.multiple_of(ROWS * b, ROWS), ROWS)
        inner = pl.ds(pl.multiple_of(EDGE + ROWS * b, EDGE), ROWS)
        low = pltpu.make_async_remote_copy(
            src_ref=x_ref.at[pl.ds(Z - 2, 2), rows], dst_ref=cells.at[pl.ds(0, 2), inner], send_sem=z_send.at[0, b], recv_sem=z_recv.at[0, b],
            device_id={"depth": lax.rem(me + 1, DEPTH)}, device_id_type=MESH,
        )
        high = pltpu.make_async_remote_copy(
            src_ref=x_ref.at[pl.ds(0, 2), rows], dst_ref=cells.at[pl.ds(Z + 2, 2), inner], send_sem=z_send.at[1, b], recv_sem=z_recv.at[1, b],
            device_id={"depth": lax.rem(me + DEPTH - 1, DEPTH)}, device_id_type=MESH,
        )
        return low, high

    x_up = remote(row_pack.at[1], row_halo.at[0], x_send, x_recv, 0, "ix", lax.rem(ix + 1, n_ix))
    x_dn = remote(row_pack.at[0], row_halo.at[1], x_send, x_recv, 1, "ix", lax.rem(ix + n_ix - 1, n_ix))

    def y_copies(b):
        low = pltpu.make_async_remote_copy(
            src_ref=pack.at[1, b], dst_ref=halo.at[0, b], send_sem=y_send.at[0, b], recv_sem=y_recv.at[0, b],
            device_id={"iy": lax.rem(iy + 1, n_iy)}, device_id_type=MESH,
        )
        high = pltpu.make_async_remote_copy(
            src_ref=pack.at[0, b], dst_ref=halo.at[1, b], send_sem=y_send.at[1, b], recv_sem=y_recv.at[1, b],
            device_id={"iy": lax.rem(iy + n_iy - 1, n_iy)}, device_id_type=MESH,
        )
        return low, high


    @pl.when(jnp.logical_not(front))
    def _():
        cells[0:2] = jnp.zeros((2,) + cells.shape[1:], BF16)

    @pl.when(jnp.logical_not(back))
    def _():
        cells[Z + 2 : Z + 4] = jnp.zeros((2,) + cells.shape[1:], BF16)


    fill_matrices(y_mat, zx_mat, pick, spread)
    for side, has in ((0, left), (1, right)):

        @pl.when(jnp.logical_not(has))
        def _(side=side):
            halo[side] = jnp.zeros(halo.shape[1:], BF16)

    for side, has in ((0, up), (1, down)):

        @pl.when(jnp.logical_not(has))
        def _(side=side):
            row_halo[side] = jnp.zeros(row_halo.shape[1:], BF16)

    lane = lax.broadcasted_iota(jnp.int32, (16, 128), 1)

    def pack_columns(b, half):
        rows = pl.ds(pl.multiple_of(EDGE + ROWS * b + 16 * half, EDGE), 16)
        first, last = jnp.zeros((16, 128), F32), jnp.zeros((16, 128), F32)
        for z in range(Z):
            ends = jnp.where(lane < 2, cells[2 + z, rows, :128].astype(F32), cells[2 + z, rows, Y - 128 :].astype(F32))
            moved = pltpu.roll(ends, 2 * z, axis=1) if z else ends
            first = jnp.where(lane >> 1 == z, moved, first)
            last = jnp.where(lane >> 1 == (z + 63) & 63, moved, last)
        last = pltpu.roll(last, 2, axis=1)
        at = pl.ds(pl.multiple_of(16 * half, 16), 16)
        pack[0, b, at] = first.astype(BF16)
        pack[1, b, at] = last.astype(BF16)

    def pack_block(i, _):
        b = lax.rem(me + 1 + i, DEPTH)
        load(b).wait()

        def one(half, _):
            pack_columns(b, half)
            return 0

        lax.fori_loop(0, 2, one, 0)
        return 0

    lax.fori_loop(0, DEPTH, pack_block, 0)
    for side, row in ((0, EDGE), (1, X)):
        for c in range(Z // 8):
            tiles = cells[2 + 8 * c : 10 + 8 * c, row : row + 16].reshape(128, Y)
            picked = jnp.dot(pick[side], tiles, preferred_element_type=F32)
            row_pack[side, 16 * c : 16 * c + 16] = picked.astype(BF16)

    pl.semaphore_wait(barrier, DEPTH - 1 + 4)

    def send_edges(i, _):
        b = lax.rem(me + 1 + i, DEPTH)
        for copies, to_high, to_low in ((z_copies(b), back, front), (y_copies(b), right, left)):
            pl.when(to_high)(copies[0].start)
            pl.when(to_low)(copies[1].start)
        return 0

    send_edges(0, 0)
    pl.when(down)(x_up.start)
    pl.when(up)(x_dn.start)
    lax.fori_loop(1, DEPTH, send_edges, 0)

    def wait_front(b):
        low, high = y_copies(b)
        pl.when(left)(low.wait_recv)
        pl.when(right)(high.wait_recv)
        pl.when(front)(z_copies(b)[0].wait_recv)
        for side, has, copy, at, row in ((0, up, x_up, 0, 0), (1, down, x_dn, DEPTH - 1, X + EDGE)):

            @pl.when(b == at)
            def _(side=side, has=has, copy=copy, row=row):
                pl.when(has)(copy.wait_recv)
                for c in range(Z // 8):
                    tiles = jnp.dot(spread[side], row_halo[side, 16 * c : 16 * c + 16], preferred_element_type=F32)
                    cells[2 + 8 * c : 10 + 8 * c, row : row + 16] = tiles.astype(BF16).reshape(8, 16, Y)

    def wait_back(b):
        pl.when(back)(z_copies(b)[1].wait_recv)

    wait_front(lax.rem(me + 1, DEPTH))

    slots = tuple(zip(slopes[:4], slopes[4:]))

    def place(n):
        return lax.rem(me + 1 + (n >> 3), DEPTH), n & 7

    def slopes_y(n, first):
        b, c = place(n)
        inner = pl.ds(pl.multiple_of(EDGE + ROWS * b, EDGE), ROWS)
        sides = jnp.concatenate([halo[0, b], halo[1, b]], axis=1)
        layer_of = (lax.broadcasted_iota(jnp.int32, (ROWS, 256), 1) & 127) >> 1
        outer = jnp.stack([jnp.where(layer_of == 8 * c + i, sides, jnp.zeros_like(sides)) for i in range(16)])
        tiles = cells[pl.ds(2 + 8 * c, 16), inner].reshape(16 * ROWS, Y)
        gy = jnp.dot(tiles, y_mat[:Y], preferred_element_type=F32)
        gy += jnp.dot(outer.reshape(16 * ROWS, 256), y_mat[Y:], preferred_element_type=F32)
        gy = gy.reshape(2, 8, ROWS, Y)
        slots[first][0][...] = gy[0]
        slots[first + 1][0][...] = gy[1]

    def slopes_zx(n, slot, j):
        b, c = place(n)
        z = 8 * c + 2 * j
        wide = pl.ds(pl.multiple_of(ROWS * b, ROWS), ROWS + 2 * EDGE)
        inner = pl.ds(pl.multiple_of(EDGE + ROWS * b, EDGE), ROWS)
        tiles = [cells[z, inner], cells[z + 1, inner], cells[z + 2, wide], cells[z + 3, wide], cells[z + 4, inner], cells[z + 5, inner]]
        g = jnp.dot(zx_mat[...], jnp.concatenate(tiles, axis=0), preferred_element_type=F32)
        slots[slot][1][:, 2 * j : 2 * j + 2] = g.reshape(3, 2, ROWS, Y)

    def march(n, slot, s):
        b, c = place(n)
        gy_ref, g_ref = slots[slot]
        row, lane = (s // 2) * 16, (s % 2) * 128
        rs, ls = slice(row, row + 16), slice(lane, lane + 128)
        inner = pl.ds(pl.multiple_of(EDGE + ROWS * b + row, EDGE), 16)
        t, w_sum, r_sum, g_sum = (parts[b, k, rs, ls] for k in range(4))
        for i in range(8):
            d = cells[2 + 8 * c + i, inner, ls].astype(F32)
            gx, gz, gy = g_ref[0, i, rs, ls], g_ref[1, i, rs, ls], gy_ref[i, rs, ls]
            s25 = g_ref[2, i, rs, ls] + 16.0 * gy
            n2 = gx * gx + gz * gz + (gy * gy + 144.0)
            bright = jnp.abs(s25) * lax.rsqrt(n2) + BASE
            grow = jnp.exp2(d * EXP2_2D)
            k5 = grow + pltpu.reciprocal(grow, approx=True)
            t_next = t * jnp.exp2(k5 * EXP2_K)
            w = (t - t_next) * bright
            t = t_next
            w_sum = w_sum + w
            r_sum = r_sum + w * jnp.tanh(d)
            g_sum = g_sum + w * jnp.exp2(d * (d * EXP2_SQ))
        for k, v in enumerate((t, w_sum, r_sum, g_sum)):
            parts[b, k, rs, ls] = v

    def send(b):
        return pltpu.make_async_remote_copy(
            src_ref=parts.at[b], dst_ref=got.at[me], send_sem=send_sem.at[b], recv_sem=recv_sem.at[me],
            device_id={"depth": b}, device_id_type=MESH,
        )

    slopes_y(0, 0)
    for q in range(2):
        for j in range(4):
            slopes_zx(q, q, j)

    def half_block(k, _):
        b = lax.rem(me + 1 + (k >> 1), DEPTH)

        @pl.when((k & 1) == 0)
        def _():
            parts[b, 0] = jnp.ones((ROWS, Y), F32)
            for i in (1, 2, 3):
                parts[b, i] = jnp.zeros((ROWS, Y), F32)

        @pl.when((k & 1) == 1)
        def _():
            wait_back(b)

        @pl.when(jnp.logical_and((k & 1) == 1, k < 2 * DEPTH - 1))
        def _():
            wait_front(lax.rem(b + 1, DEPTH))

        for h in range(2):
            @pl.when(k + me >= 0)
            def _(h=h):
                n = 4 * k + 2 * h
                use, fill = 2 * h, 2 - 2 * h
                slopes_y(n + 2, fill)
                for i in range(8):
                    slopes_zx(n + 2 + i // 4, fill + i // 4, i % 4)
                    march(n + i % 2, use + i % 2, i // 2)

        @pl.when(jnp.logical_and((k & 1) == 1, k < 2 * DEPTH - 2))
        def _():
            send(b).start()

        return 0

    lax.fori_loop(0, 2 * DEPTH, half_block, 0)

    got[me] = parts[me]
    for step in range(1, DEPTH):
        src = lax.rem(me + step, DEPTH)
        pltpu.make_async_remote_copy(
            src_ref=parts.at[src], dst_ref=got.at[src], send_sem=send_sem.at[src], recv_sem=recv_sem.at[src],
            device_id={"depth": src}, device_id_type=MESH,
        ).wait_recv()

    through = got[0, 0]
    w_sum, r_sum, g_sum = got[0, 1], got[0, 2], got[0, 3]
    for i in range(1, DEPTH):
        w_sum += through * got[i, 1]
        r_sum += through * got[i, 2]
        g_sum += through * got[i, 3]
        through = through * got[i, 0]
    out_ref[0] = (w_sum + r_sum) * (0.5 * 0.7 / 25.0)
    out_ref[1] = g_sum * (0.7 / 25.0)
    out_ref[2] = (w_sum - r_sum) * (0.5 * 0.7 / 25.0)
    out_ref[3] = 1.0 - through

    for step in range(1, DEPTH):
        send(lax.rem(me + step, DEPTH)).wait_send()
    for has, copy in ((down, x_up), (up, x_dn)):
        pl.when(has)(copy.wait_send)

    def sent_edges(b, _):
        for copies, to_high, to_low in ((z_copies(b), back, front), (y_copies(b), right, left)):
            pl.when(to_high)(copies[0].wait_send)
            pl.when(to_low)(copies[1].wait_send)
        return 0

    lax.fori_loop(0, DEPTH, sent_edges, 0)


def on_device(density):
    vmem, dma = pl.BlockSpec(memory_space=pltpu.VMEM), pltpu.SemaphoreType.DMA
    return pl.pallas_call(
        kernel,
        out_shape=jax.ShapeDtypeStruct((4, ROWS, Y), F32),
        in_specs=[pl.BlockSpec(memory_space=pl.ANY)],
        out_specs=vmem,
        scratch_shapes=[
            pltpu.VMEM((Y + 256, Y), BF16),
            pltpu.VMEM((6 * ROWS, 256), BF16),
            pltpu.VMEM((2, 16, 128), BF16),
            pltpu.VMEM((2, 128, 16), BF16),
            pltpu.VMEM((Z + 4, X + 2 * EDGE, Y), BF16),
            pltpu.VMEM((2, DEPTH, ROWS, 128), BF16),
            pltpu.VMEM((2, DEPTH, ROWS, 128), BF16),
            pltpu.VMEM((2, 2 * Z, Y), BF16),
            pltpu.VMEM((2, 2 * Z, Y), BF16),
            pltpu.VMEM((DEPTH, 4, ROWS, Y), F32),
            pltpu.VMEM((DEPTH, 4, ROWS, Y), F32),
        ]
        + [dma((DEPTH,))]
        + [dma((2, DEPTH))] * 2
        + [dma((2,))] * 2
        + [dma((2, DEPTH))] * 2
        + [dma((DEPTH,))] * 2
        + [pltpu.VMEM((8, ROWS, Y), F32)] * 4
        + [pltpu.VMEM((3, 8, ROWS, Y), F32)] * 4,
        compiler_params=pltpu.CompilerParams(collective_id=0, has_side_effects=True, vmem_limit_bytes=48 << 20),
        name="render",
    )(density)


def solution(mesh):
    return jax.shard_map(
        on_device,
        mesh=mesh,
        in_specs=(P("depth", "ix", "iy"),),
        out_specs=P(None, ("ix", "depth"), "iy"),
        check_vma=False,
    )
```

```python
import jax
import jax.numpy as jnp
import numpy as np
from jax import lax
from jax.experimental import pallas as pl
from jax.experimental.pallas import tpu as pltpu
from jax.sharding import PartitionSpec as P

MESH = pl.DeviceIdType.MESH
F32, BF16 = jnp.float32, jnp.bfloat16
Z, X, Y = 64, 256, 256
DEPTH = 8
ROWS = X // DEPTH
EDGE = 16
NZ = 512
LAG = 3
EXP2_2D = float(2.0 * np.log2(np.e))
EXP2_K = float(-0.1 * np.log2(np.e) / NZ)
EXP2_SQ = float(-np.log2(np.e))
SCALE = 0.7 * 16.0 / 25.0
BASE = 0.3 / SCALE


def tap(step):
    near = jnp.where(step == 1, 8.0, jnp.where(step == -1, -8.0, 0.0))
    return jnp.where(step == 2, -1.0, jnp.where(step == -2, 1.0, near))


def fill_matrices(y_mat, zx_mat, pick, spread):
    k, y = (lax.broadcasted_iota(jnp.int32, (256, Y), i) for i in (0, 1))
    y_mat[:256] = tap(k - y).astype(BF16)
    y_mat[256:] = tap(jnp.where(k < 128, (k & 1) - 2, Y + (k & 1)) - y).astype(BF16)
    m, c = (lax.broadcasted_iota(jnp.int32, (2 * ROWS, 256), i) for i in (0, 1))
    layer, row = m >> 5, m & 31
    at = jnp.where(c < 64, c >> 5, jnp.where(c < 192, 1 + (c >> 6), (c >> 5) - 2))
    across = jnp.where((c >= 64) & (c < 192), (c & 63) - EDGE, c & 31)
    gx = jnp.where(at == layer + 2, tap(across - row), 0.0)
    gz = jnp.where(across == row, tap(at - 2 - layer), 0.0)
    for i, g in enumerate((gx, gz, (15.0 / 16.0) * gx + (12.0 / 16.0) * gz)):
        zx_mat[2 * ROWS * i : 2 * ROWS * (i + 1)] = g.astype(BF16)
    m, c = (lax.broadcasted_iota(jnp.int32, (16, 128), i) for i in (0, 1))
    o, q = (lax.broadcasted_iota(jnp.int32, (128, 16), i) for i in (0, 1))
    for side, start in ((0, 0), (1, 14)):
        pick[side] = jnp.where(((c >> 4) == (m >> 1)) & ((c & 15) == start + (m & 1)), 1.0, 0.0).astype(BF16)
        spread[1 - side] = jnp.where(((o >> 4) == (q >> 1)) & ((o & 15) == start + (q & 1)), 1.0, 0.0).astype(BF16)


def kernel(
    x_ref, out_ref,
    y_mat, zx_mat, pick, spread, cells, halo, pack, row_pack, row_halo, parts, got,
    load_sem, z_send, z_recv, x_send, x_recv, y_send, y_recv, send_sem, recv_sem, *slopes,
):
    me = lax.axis_index("depth")
    ix, iy = lax.axis_index("ix"), lax.axis_index("iy")
    n_ix, n_iy = lax.axis_size("ix"), lax.axis_size("iy")
    front, back = me > 0, me < DEPTH - 1
    up, down = ix > 0, ix < n_ix - 1
    left, right = iy > 0, iy < n_iy - 1

    def block(i, at=me):
        swap = jnp.where(at == 7, 1, jnp.where(at == 6, 2, 0))
        return lax.rem(at + 1 + jnp.where(i <= swap, swap - i, i), DEPTH)

    def load(b):
        rows = pl.ds(pl.multiple_of(ROWS * b, ROWS), ROWS)
        inner = pl.ds(pl.multiple_of(EDGE + ROWS * b, EDGE), ROWS)
        return pltpu.make_async_copy(x_ref.at[:, rows], cells.at[pl.ds(2, Z), inner], load_sem.at[b])

    barrier = pltpu.get_barrier_semaphore()
    for step in range(1, DEPTH):
        pl.semaphore_signal(barrier, inc=1, device_id={"depth": lax.rem(me + step, DEPTH)}, device_id_type=MESH)
    for axis, at, count in (("ix", ix, n_ix), ("iy", iy, n_iy)):
        for step in (1, count - 1):
            pl.semaphore_signal(barrier, inc=1, device_id={axis: lax.rem(at + step, count)}, device_id_type=MESH)
    for i in range(DEPTH):
        load(block(i)).start()

    def remote(src, dst, sems, recvs, k, axis, to):
        return pltpu.make_async_remote_copy(
            src_ref=src, dst_ref=dst, send_sem=sems.at[k], recv_sem=recvs.at[k],
            device_id={axis: to}, device_id_type=MESH,
        )

    def z_copies(b):
        rows = pl.ds(pl.multiple_of(ROWS * b, ROWS), ROWS)
        inner = pl.ds(pl.multiple_of(EDGE + ROWS * b, EDGE), ROWS)
        low = pltpu.make_async_remote_copy(
            src_ref=x_ref.at[pl.ds(Z - 2, 2), rows], dst_ref=cells.at[pl.ds(0, 2), inner], send_sem=z_send.at[0, b], recv_sem=z_recv.at[0, b],
            device_id={"depth": lax.rem(me + 1, DEPTH)}, device_id_type=MESH,
        )
        high = pltpu.make_async_remote_copy(
            src_ref=x_ref.at[pl.ds(0, 2), rows], dst_ref=cells.at[pl.ds(Z + 2, 2), inner], send_sem=z_send.at[1, b], recv_sem=z_recv.at[1, b],
            device_id={"depth": lax.rem(me + DEPTH - 1, DEPTH)}, device_id_type=MESH,
        )
        return low, high

    x_up = remote(row_pack.at[1], row_halo.at[0], x_send, x_recv, 0, "ix", lax.rem(ix + 1, n_ix))
    x_dn = remote(row_pack.at[0], row_halo.at[1], x_send, x_recv, 1, "ix", lax.rem(ix + n_ix - 1, n_ix))

    def y_copies(b):
        low = pltpu.make_async_remote_copy(
            src_ref=pack.at[1, b], dst_ref=halo.at[0, b], send_sem=y_send.at[0, b], recv_sem=y_recv.at[0, b],
            device_id={"iy": lax.rem(iy + 1, n_iy)}, device_id_type=MESH,
        )
        high = pltpu.make_async_remote_copy(
            src_ref=pack.at[0, b], dst_ref=halo.at[1, b], send_sem=y_send.at[1, b], recv_sem=y_recv.at[1, b],
            device_id={"iy": lax.rem(iy + n_iy - 1, n_iy)}, device_id_type=MESH,
        )
        return low, high


    @pl.when(jnp.logical_not(front))
    def _():
        cells[0:2] = jnp.zeros((2,) + cells.shape[1:], BF16)

    @pl.when(jnp.logical_not(back))
    def _():
        cells[Z + 2 : Z + 4] = jnp.zeros((2,) + cells.shape[1:], BF16)


    fill_matrices(y_mat, zx_mat, pick, spread)
    for side, has in ((0, left), (1, right)):

        @pl.when(jnp.logical_not(has))
        def _(side=side):
            halo[side] = jnp.zeros(halo.shape[1:], BF16)

    for side, has in ((0, up), (1, down)):

        @pl.when(jnp.logical_not(has))
        def _(side=side):
            row_halo[side] = jnp.zeros(row_halo.shape[1:], BF16)

    lane = lax.broadcasted_iota(jnp.int32, (16, 128), 1)

    def pack_columns(b, half):
        rows = pl.ds(pl.multiple_of(EDGE + ROWS * b + 16 * half, EDGE), 16)
        first, last = jnp.zeros((16, 128), F32), jnp.zeros((16, 128), F32)
        for z in range(Z):
            ends = jnp.where(lane < 2, cells[2 + z, rows, :128].astype(F32), cells[2 + z, rows, Y - 128 :].astype(F32))
            moved = pltpu.roll(ends, 2 * z, axis=1) if z else ends
            first = jnp.where(lane >> 1 == z, moved, first)
            last = jnp.where(lane >> 1 == (z + 63) & 63, moved, last)
        last = pltpu.roll(last, 2, axis=1)
        at = pl.ds(pl.multiple_of(16 * half, 16), 16)
        pack[0, b, at] = first.astype(BF16)
        pack[1, b, at] = last.astype(BF16)

    def pack_block(i, _):
        b = block(i)
        load(b).wait()

        def one(half, _):
            pack_columns(b, half)
            return 0

        lax.fori_loop(0, 2, one, 0)
        return 0

    lax.fori_loop(0, DEPTH, pack_block, 0)
    for side, row in ((0, EDGE), (1, X)):
        for c in range(Z // 8):
            tiles = cells[2 + 8 * c : 10 + 8 * c, row : row + 16].reshape(128, Y)
            picked = jnp.dot(pick[side], tiles, preferred_element_type=F32)
            row_pack[side, 16 * c : 16 * c + 16] = picked.astype(BF16)

    slots = tuple(zip(slopes[:4], slopes[4:]))

    def place(n):
        return block(n >> 3), n & 7

    def slopes_y(n, first):
        b, c = place(n)
        inner = pl.ds(pl.multiple_of(EDGE + ROWS * b, EDGE), ROWS)
        sides = jnp.concatenate([halo[0, b], halo[1, b]], axis=1)
        layer_of = (lax.broadcasted_iota(jnp.int32, (ROWS, 256), 1) & 127) >> 1
        outer = jnp.stack([jnp.where(layer_of == 8 * c + i, sides, jnp.zeros_like(sides)) for i in range(16)])
        tiles = cells[pl.ds(2 + 8 * c, 16), inner].reshape(16 * ROWS, Y)
        gy = jnp.dot(tiles, y_mat[:Y], preferred_element_type=F32)
        gy += jnp.dot(outer.reshape(16 * ROWS, 256), y_mat[Y:], preferred_element_type=F32)
        gy = gy.reshape(2, 8, ROWS, Y)
        slots[first][0][...] = gy[0]
        slots[first + 1][0][...] = gy[1]

    def slopes_zx(n, slot, j):
        b, c = place(n)
        z = 8 * c + 2 * j
        wide = pl.ds(pl.multiple_of(ROWS * b, ROWS), ROWS + 2 * EDGE)
        inner = pl.ds(pl.multiple_of(EDGE + ROWS * b, EDGE), ROWS)
        tiles = [cells[z, inner], cells[z + 1, inner], cells[z + 2, wide], cells[z + 3, wide], cells[z + 4, inner], cells[z + 5, inner]]
        g = jnp.dot(zx_mat[...], jnp.concatenate(tiles, axis=0), preferred_element_type=F32)
        slots[slot][1][:, 2 * j : 2 * j + 2] = g.reshape(3, 2, ROWS, Y)

    for j in range(1, 8):
        slopes_zx(j // 4, j // 4, j % 4)

    pl.semaphore_wait(barrier, DEPTH - 1 + 4)

    def send_layers(i, _):
        pl.when(back)(z_copies(block(i, me + 1))[0].start)
        pl.when(front)(z_copies(block(i, me - 1))[1].start)
        return 0

    def send_columns(i, _):
        low, high = y_copies(block(i))
        pl.when(right)(low.start)
        pl.when(left)(high.start)
        return 0

    send_columns(0, 0)
    send_layers(0, 0)
    pl.when(down)(x_up.start)
    pl.when(up)(x_dn.start)

    def send_rest(i, _):
        send_columns(i, 0)
        return send_layers(i, 0)

    lax.fori_loop(1, DEPTH, send_rest, 0)

    def wait_front(b):
        low, high = y_copies(b)
        pl.when(left)(low.wait_recv)
        pl.when(right)(high.wait_recv)
        pl.when(front)(z_copies(b)[0].wait_recv)
        for side, has, copy, at, row in ((0, up, x_up, 0, 0), (1, down, x_dn, DEPTH - 1, X + EDGE)):

            @pl.when(b == at)
            def _(side=side, has=has, copy=copy, row=row):
                pl.when(has)(copy.wait_recv)
                for c in range(Z // 8):
                    tiles = jnp.dot(spread[side], row_halo[side, 16 * c : 16 * c + 16], preferred_element_type=F32)
                    cells[2 + 8 * c : 10 + 8 * c, row : row + 16] = tiles.astype(BF16).reshape(8, 16, Y)

    def wait_back(b):
        pl.when(back)(z_copies(b)[1].wait_recv)

    wait_front(block(0))

    def march(n, slot, s, after):
        b, c = place(n)
        gy_ref, g_ref = slots[slot]
        row, lane = (s // 2) * 16, (s % 2) * 128
        rs, ls = slice(row, row + 16), slice(lane, lane + 128)
        inner = pl.ds(pl.multiple_of(EDGE + ROWS * b + row, EDGE), 16)
        t, w_sum, r_sum, g_sum = (parts[b, k, rs, ls] for k in range(4))
        for ref in after:
            t = t + 0.0 * ref[rs, ls]
        for i in range(8):
            d = cells[2 + 8 * c + i, inner, ls].astype(F32)
            gx, gz, gy = g_ref[0, i, rs, ls], g_ref[1, i, rs, ls], gy_ref[i, rs, ls]
            along = g_ref[2, i, rs, ls] + gy
            n2 = gx * gx + gz * gz + (gy * gy + 144.0)
            bright = jnp.abs(along) * lax.rsqrt(n2) + BASE
            grow = jnp.exp2(d * EXP2_2D)
            k5 = grow + pltpu.reciprocal(grow, approx=True)
            t_next = t * jnp.exp2(k5 * EXP2_K)
            w = (t - t_next) * bright
            t = t_next
            w_sum = w_sum + w
            r_sum = r_sum + w * jnp.tanh(d)
            g_sum = g_sum + w * jnp.exp2(d * (d * EXP2_SQ))
        for k, v in enumerate((t, w_sum, r_sum, g_sum)):
            parts[b, k, rs, ls] = v

    def send(b):
        return pltpu.make_async_remote_copy(
            src_ref=parts.at[b], dst_ref=got.at[me], send_sem=send_sem.at[b], recv_sem=recv_sem.at[me],
            device_id={"depth": b}, device_id_type=MESH,
        )

    slopes_zx(0, 0, 0)
    slopes_y(0, 0)

    def turn(m, _):
        i, quarter = m >> 2, m & 3
        b = block(i)

        @pl.when(quarter == 0)
        def _():
            parts[b, 0] = jnp.ones((ROWS, Y), F32)
            for p in (1, 2, 3):
                parts[b, p] = jnp.zeros((ROWS, Y), F32)

        pl.when(quarter == 2)(lambda: wait_back(b))
        pl.when(jnp.logical_and(quarter == 3, i < DEPTH - 1))(lambda: wait_front(block(i + 1)))

        for h in range(2):

            @pl.when((m & 1) == h)
            def _(h=h):
                use, fill = 2 * h, 2 - 2 * h
                slopes_y(2 * m + 2, fill)
                for p in range(8):
                    slopes_zx(2 * m + 2 + p // 4, fill + p // 4, p % 4)
                    after = [slots[fill + (p - LAG) // 4][1].at[0, 2 * ((p - LAG) % 4)]] if p >= LAG else []
                    if p in (5, 6):
                        after.append(slots[fill + (p == ((5, 6))[1])][0].at[7])
                    march(2 * m + p % 2, use + p % 2, p // 2, after)

        @pl.when(jnp.logical_and(quarter == 3, i < DEPTH - 1))
        def _():
            send(b).start()

        return 0

    lax.fori_loop(0, 4 * DEPTH, turn, 0)

    got[me] = parts[me]
    for step in range(1, DEPTH):
        src = lax.rem(me + step, DEPTH)
        pltpu.make_async_remote_copy(
            src_ref=parts.at[src], dst_ref=got.at[src], send_sem=send_sem.at[src], recv_sem=recv_sem.at[src],
            device_id={"depth": src}, device_id_type=MESH,
        ).wait_recv()

    through = got[0, 0]
    w_sum, r_sum, g_sum = got[0, 1], got[0, 2], got[0, 3]
    for i in range(1, DEPTH):
        w_sum += through * got[i, 1]
        r_sum += through * got[i, 2]
        g_sum += through * got[i, 3]
        through = through * got[i, 0]
    out_ref[0] = (w_sum + r_sum) * (0.5 * SCALE)
    out_ref[1] = g_sum * SCALE
    out_ref[2] = (w_sum - r_sum) * (0.5 * SCALE)
    out_ref[3] = 1.0 - through

    for step in range(1, DEPTH):
        send(lax.rem(me + step, DEPTH)).wait_send()
    for has, copy in ((down, x_up), (up, x_dn)):
        pl.when(has)(copy.wait_send)

    def sent_edges(b, _):
        for copies, to_high, to_low in ((z_copies(b), back, front), (y_copies(b), right, left)):
            pl.when(to_high)(copies[0].wait_send)
            pl.when(to_low)(copies[1].wait_send)
        return 0

    lax.fori_loop(0, DEPTH, sent_edges, 0)


def on_device(density):
    vmem, dma = pl.BlockSpec(memory_space=pltpu.VMEM), pltpu.SemaphoreType.DMA
    return pl.pallas_call(
        kernel,
        out_shape=jax.ShapeDtypeStruct((4, ROWS, Y), F32),
        in_specs=[pl.BlockSpec(memory_space=pl.ANY)],
        out_specs=vmem,
        scratch_shapes=[
            pltpu.VMEM((Y + 256, Y), BF16),
            pltpu.VMEM((6 * ROWS, 256), BF16),
            pltpu.VMEM((2, 16, 128), BF16),
            pltpu.VMEM((2, 128, 16), BF16),
            pltpu.VMEM((Z + 4, X + 2 * EDGE, Y), BF16),
            pltpu.VMEM((2, DEPTH, ROWS, 128), BF16),
            pltpu.VMEM((2, DEPTH, ROWS, 128), BF16),
            pltpu.VMEM((2, 2 * Z, Y), BF16),
            pltpu.VMEM((2, 2 * Z, Y), BF16),
            pltpu.VMEM((DEPTH, 4, ROWS, Y), F32),
            pltpu.VMEM((DEPTH, 4, ROWS, Y), F32),
        ]
        + [dma((DEPTH,))]
        + [dma((2, DEPTH))] * 2
        + [dma((2,))] * 2
        + [dma((2, DEPTH))] * 2
        + [dma((DEPTH,))] * 2
        + [pltpu.VMEM((8, ROWS, Y), F32)] * 4
        + [pltpu.VMEM((3, 8, ROWS, Y), F32)] * 4,
        compiler_params=pltpu.CompilerParams(collective_id=0, has_side_effects=True, vmem_limit_bytes=48 << 20),
        name="render",
    )(density)


def solution(mesh):
    return jax.shard_map(
        on_device,
        mesh=mesh,
        in_specs=(P("depth", "ix", "iy"),),
        out_specs=P(None, ("ix", "depth"), "iy"),
        check_vma=False,
    )
```

```python
import jax
import jax.numpy as jnp
import numpy as np
from jax import lax
from jax.experimental import pallas as pl
from jax.experimental.pallas import tpu as pltpu
from jax.sharding import PartitionSpec as P

MESH = pl.DeviceIdType.MESH
F32, BF16 = jnp.float32, jnp.bfloat16
Z, X, Y = 64, 256, 256
DEPTH = 8
ROWS = X // DEPTH
EDGE = 16
NZ = 512
LAG = 3
EXP2_2D = float(2.0 * np.log2(np.e))
EXP2_K = float(-0.1 * np.log2(np.e) / NZ)
EXP2_SQ = float(-np.log2(np.e))
SCALE = 0.7 * 16.0 / 25.0
BASE = 0.3 / SCALE


def tap(step):
    near = jnp.where(step == 1, 8.0, jnp.where(step == -1, -8.0, 0.0))
    return jnp.where(step == 2, -1.0, jnp.where(step == -2, 1.0, near))


def fill_matrices(y_mat, zx_mat, pick, spread):
    k, y = (lax.broadcasted_iota(jnp.int32, (256, Y), i) for i in (0, 1))
    y_mat[:256] = tap(k - y).astype(BF16)
    y_mat[256:] = tap(jnp.where(k < 128, (k & 1) - 2, Y + (k & 1)) - y).astype(BF16)
    m, c = (lax.broadcasted_iota(jnp.int32, (2 * ROWS, 256), i) for i in (0, 1))
    layer, row = m >> 5, m & 31
    at = jnp.where(c < 64, c >> 5, jnp.where(c < 192, 1 + (c >> 6), (c >> 5) - 2))
    across = jnp.where((c >= 64) & (c < 192), (c & 63) - EDGE, c & 31)
    gx = jnp.where(at == layer + 2, tap(across - row), 0.0)
    gz = jnp.where(across == row, tap(at - 2 - layer), 0.0)
    for i, g in enumerate((gx, gz, (15.0 / 16.0) * gx + (12.0 / 16.0) * gz)):
        zx_mat[2 * ROWS * i : 2 * ROWS * (i + 1)] = g.astype(BF16)
    m, c = (lax.broadcasted_iota(jnp.int32, (16, 128), i) for i in (0, 1))
    o, q = (lax.broadcasted_iota(jnp.int32, (128, 16), i) for i in (0, 1))
    for side, start in ((0, 0), (1, 14)):
        pick[side] = jnp.where(((c >> 4) == (m >> 1)) & ((c & 15) == start + (m & 1)), 1.0, 0.0).astype(BF16)
        spread[1 - side] = jnp.where(((o >> 4) == (q >> 1)) & ((o & 15) == start + (q & 1)), 1.0, 0.0).astype(BF16)


def kernel(
    x_ref, out_ref,
    y_mat, zx_mat, pick, spread, cells, halo, pack, row_pack, row_halo, parts, got,
    load_sem, z_send, z_recv, x_send, x_recv, y_send, y_recv, send_sem, recv_sem, *slopes,
):
    me = lax.axis_index("depth")
    ix, iy = lax.axis_index("ix"), lax.axis_index("iy")
    n_ix, n_iy = lax.axis_size("ix"), lax.axis_size("iy")
    front, back = me > 0, me < DEPTH - 1
    up, down = ix > 0, ix < n_ix - 1
    left, right = iy > 0, iy < n_iy - 1

    def block(i, at=me):
        swapped = jnp.where(jnp.logical_and(jnp.logical_or(at == 0, at == DEPTH - 1), i < 2), 1 - i, i)
        return lax.rem(jnp.where((at & 1) == 1, at + 1 + swapped, at + 2 * DEPTH - 1 - swapped), DEPTH)

    def load(b):
        rows = pl.ds(pl.multiple_of(ROWS * b, ROWS), ROWS)
        inner = pl.ds(pl.multiple_of(EDGE + ROWS * b, EDGE), ROWS)
        return pltpu.make_async_copy(x_ref.at[:, rows], cells.at[pl.ds(2, Z), inner], load_sem.at[b])

    barrier = pltpu.get_barrier_semaphore()
    for step in range(1, DEPTH):
        pl.semaphore_signal(barrier, inc=1, device_id={"depth": lax.rem(me + step, DEPTH)}, device_id_type=MESH)
    for axis, at, count in (("ix", ix, n_ix), ("iy", iy, n_iy)):
        for step in (1, count - 1):
            pl.semaphore_signal(barrier, inc=1, device_id={axis: lax.rem(at + step, count)}, device_id_type=MESH)
    for i in range(DEPTH):
        load(block(i)).start()

    def remote(src, dst, sems, recvs, k, axis, to):
        return pltpu.make_async_remote_copy(
            src_ref=src, dst_ref=dst, send_sem=sems.at[k], recv_sem=recvs.at[k],
            device_id={axis: to}, device_id_type=MESH,
        )

    def z_copies(b):
        rows = pl.ds(pl.multiple_of(ROWS * b, ROWS), ROWS)
        inner = pl.ds(pl.multiple_of(EDGE + ROWS * b, EDGE), ROWS)
        low = pltpu.make_async_remote_copy(
            src_ref=x_ref.at[pl.ds(Z - 2, 2), rows], dst_ref=cells.at[pl.ds(0, 2), inner], send_sem=z_send.at[0, b], recv_sem=z_recv.at[0, b],
            device_id={"depth": lax.rem(me + 1, DEPTH)}, device_id_type=MESH,
        )
        high = pltpu.make_async_remote_copy(
            src_ref=x_ref.at[pl.ds(0, 2), rows], dst_ref=cells.at[pl.ds(Z + 2, 2), inner], send_sem=z_send.at[1, b], recv_sem=z_recv.at[1, b],
            device_id={"depth": lax.rem(me + DEPTH - 1, DEPTH)}, device_id_type=MESH,
        )
        return low, high

    x_up = remote(row_pack.at[1], row_halo.at[0], x_send, x_recv, 0, "ix", lax.rem(ix + 1, n_ix))
    x_dn = remote(row_pack.at[0], row_halo.at[1], x_send, x_recv, 1, "ix", lax.rem(ix + n_ix - 1, n_ix))

    def y_copies(b):
        low = pltpu.make_async_remote_copy(
            src_ref=pack.at[1, b], dst_ref=halo.at[0, b], send_sem=y_send.at[0, b], recv_sem=y_recv.at[0, b],
            device_id={"iy": lax.rem(iy + 1, n_iy)}, device_id_type=MESH,
        )
        high = pltpu.make_async_remote_copy(
            src_ref=pack.at[0, b], dst_ref=halo.at[1, b], send_sem=y_send.at[1, b], recv_sem=y_recv.at[1, b],
            device_id={"iy": lax.rem(iy + n_iy - 1, n_iy)}, device_id_type=MESH,
        )
        return low, high


    @pl.when(jnp.logical_not(front))
    def _():
        cells[0:2] = jnp.zeros((2,) + cells.shape[1:], BF16)

    @pl.when(jnp.logical_not(back))
    def _():
        cells[Z + 2 : Z + 4] = jnp.zeros((2,) + cells.shape[1:], BF16)


    fill_matrices(y_mat, zx_mat, pick, spread)
    for side, has in ((0, left), (1, right)):

        @pl.when(jnp.logical_not(has))
        def _(side=side):
            halo[side] = jnp.zeros(halo.shape[1:], BF16)

    for side, has in ((0, up), (1, down)):

        @pl.when(jnp.logical_not(has))
        def _(side=side):
            row_halo[side] = jnp.zeros(row_halo.shape[1:], BF16)

    lane = lax.broadcasted_iota(jnp.int32, (16, 128), 1)

    def pack_columns(b, half):
        rows = pl.ds(pl.multiple_of(EDGE + ROWS * b + 16 * half, EDGE), 16)
        first, last = jnp.zeros((16, 128), F32), jnp.zeros((16, 128), F32)
        for z in range(Z):
            ends = jnp.where(lane < 2, cells[2 + z, rows, :128].astype(F32), cells[2 + z, rows, Y - 128 :].astype(F32))
            moved = pltpu.roll(ends, 2 * z, axis=1) if z else ends
            first = jnp.where(lane >> 1 == z, moved, first)
            last = jnp.where(lane >> 1 == (z + 63) & 63, moved, last)
        last = pltpu.roll(last, 2, axis=1)
        at = pl.ds(pl.multiple_of(16 * half, 16), 16)
        pack[0, b, at] = first.astype(BF16)
        pack[1, b, at] = last.astype(BF16)

    def pack_block(i, _):
        b = block(i)
        load(b).wait()

        def one(half, _):
            pack_columns(b, half)
            return 0

        lax.fori_loop(0, 2, one, 0)
        return 0

    lax.fori_loop(0, DEPTH, pack_block, 0)
    for side, row in ((0, EDGE), (1, X)):
        for c in range(Z // 8):
            tiles = cells[2 + 8 * c : 10 + 8 * c, row : row + 16].reshape(128, Y)
            picked = jnp.dot(pick[side], tiles, preferred_element_type=F32)
            row_pack[side, 16 * c : 16 * c + 16] = picked.astype(BF16)

    slots = tuple(zip(slopes[:4], slopes[4:]))

    def place(n):
        return block(n >> 3), n & 7

    def slopes_y(n, first):
        b, c = place(n)
        inner = pl.ds(pl.multiple_of(EDGE + ROWS * b, EDGE), ROWS)
        sides = jnp.concatenate([halo[0, b], halo[1, b]], axis=1)
        layer_of = (lax.broadcasted_iota(jnp.int32, (ROWS, 256), 1) & 127) >> 1
        outer = jnp.stack([jnp.where(layer_of == 8 * c + i, sides, jnp.zeros_like(sides)) for i in range(16)])
        tiles = cells[pl.ds(2 + 8 * c, 16), inner].reshape(16 * ROWS, Y)
        gy = jnp.dot(tiles, y_mat[:Y], preferred_element_type=F32)
        gy += jnp.dot(outer.reshape(16 * ROWS, 256), y_mat[Y:], preferred_element_type=F32)
        gy = gy.reshape(2, 8, ROWS, Y)
        slots[first][0][...] = gy[0]
        slots[first + 1][0][...] = gy[1]

    def slopes_zx(n, slot, j):
        b, c = place(n)
        z = 8 * c + 2 * j
        wide = pl.ds(pl.multiple_of(ROWS * b, ROWS), ROWS + 2 * EDGE)
        inner = pl.ds(pl.multiple_of(EDGE + ROWS * b, EDGE), ROWS)
        tiles = [cells[z, inner], cells[z + 1, inner], cells[z + 2, wide], cells[z + 3, wide], cells[z + 4, inner], cells[z + 5, inner]]
        g = jnp.dot(zx_mat[...], jnp.concatenate(tiles, axis=0), preferred_element_type=F32)
        slots[slot][1][:, 2 * j : 2 * j + 2] = g.reshape(3, 2, ROWS, Y)

    for j in range(1, 8):
        slopes_zx(j // 4, j // 4, j % 4)

    pl.semaphore_wait(barrier, DEPTH - 1 + 4)

    def send_layers(i, _):
        pl.when(back)(z_copies(block(i, me + 1))[0].start)
        pl.when(front)(z_copies(block(i, me - 1))[1].start)
        return 0

    def send_columns(i, _):
        low, high = y_copies(block(i))
        pl.when(right)(low.start)
        pl.when(left)(high.start)
        return 0

    send_columns(0, 0)
    send_layers(0, 0)
    pl.when(down)(x_up.start)
    pl.when(up)(x_dn.start)

    def send_rest(i, _):
        send_columns(i, 0)
        return send_layers(i, 0)

    lax.fori_loop(1, DEPTH, send_rest, 0)

    def wait_front(b):
        low, high = y_copies(b)
        pl.when(left)(low.wait_recv)
        pl.when(right)(high.wait_recv)
        pl.when(front)(z_copies(b)[0].wait_recv)
        for side, has, copy, at, row in ((0, up, x_up, 0, 0), (1, down, x_dn, DEPTH - 1, X + EDGE)):

            @pl.when(b == at)
            def _(side=side, has=has, copy=copy, row=row):
                pl.when(has)(copy.wait_recv)
                for c in range(Z // 8):
                    tiles = jnp.dot(spread[side], row_halo[side, 16 * c : 16 * c + 16], preferred_element_type=F32)
                    cells[2 + 8 * c : 10 + 8 * c, row : row + 16] = tiles.astype(BF16).reshape(8, 16, Y)

    def wait_back(b):
        pl.when(back)(z_copies(b)[1].wait_recv)

    wait_front(block(0))

    def march(n, slot, s, after):
        b, c = place(n)
        gy_ref, g_ref = slots[slot]
        row, lane = (s // 2) * 16, (s % 2) * 128
        rs, ls = slice(row, row + 16), slice(lane, lane + 128)
        inner = pl.ds(pl.multiple_of(EDGE + ROWS * b + row, EDGE), 16)
        t, w_sum, r_sum, g_sum = (parts[b, k, rs, ls] for k in range(4))
        for ref in after:
            t = t + 0.0 * ref[rs, ls]
        for i in range(8):
            d = cells[2 + 8 * c + i, inner, ls].astype(F32)
            gx, gz, gy = g_ref[0, i, rs, ls], g_ref[1, i, rs, ls], gy_ref[i, rs, ls]
            along = g_ref[2, i, rs, ls] + gy
            n2 = gx * gx + gz * gz + (gy * gy + 144.0)
            bright = jnp.abs(along) * lax.rsqrt(n2) + BASE
            grow = jnp.exp2(d * EXP2_2D)
            k5 = grow + pltpu.reciprocal(grow, approx=True)
            t_next = t * jnp.exp2(k5 * EXP2_K)
            w = (t - t_next) * bright
            t = t_next
            w_sum = w_sum + w
            r_sum = r_sum + w * jnp.tanh(d)
            g_sum = g_sum + w * jnp.exp2(d * (d * EXP2_SQ))
        for k, v in enumerate((t, w_sum, r_sum, g_sum)):
            parts[b, k, rs, ls] = v

    def send(b):
        return pltpu.make_async_remote_copy(
            src_ref=parts.at[b], dst_ref=got.at[me], send_sem=send_sem.at[b], recv_sem=recv_sem.at[me],
            device_id={"depth": b}, device_id_type=MESH,
        )

    slopes_zx(0, 0, 0)
    slopes_y(0, 0)

    def turn(m, _):
        i, quarter = m >> 2, m & 3
        b = block(i)

        @pl.when(quarter == 0)
        def _():
            parts[b, 0] = jnp.ones((ROWS, Y), F32)
            for p in (1, 2, 3):
                parts[b, p] = jnp.zeros((ROWS, Y), F32)

        pl.when(quarter == 2)(lambda: wait_back(b))
        pl.when(jnp.logical_and(quarter == 3, i < DEPTH - 1))(lambda: wait_front(block(i + 1)))

        for h in range(2):

            @pl.when((m & 1) == h)
            def _(h=h):
                use, fill = 2 * h, 2 - 2 * h
                slopes_y(2 * m + 2, fill)
                for p in range(8):
                    slopes_zx(2 * m + 2 + p // 4, fill + p // 4, p % 4)
                    after = [slots[fill + (p - LAG) // 4][1].at[0, 2 * ((p - LAG) % 4)]] if p >= LAG else []
                    if p in (5, 6):
                        after.append(slots[fill + (p == ((5, 6))[1])][0].at[7])
                    march(2 * m + p % 2, use + p % 2, p // 2, after)

        @pl.when(jnp.logical_and(quarter == 3, i < DEPTH - 1))
        def _():
            send(b).start()

        return 0

    lax.fori_loop(0, 4 * DEPTH, turn, 0)

    got[me] = parts[me]
    for step in range(1, DEPTH):
        src = lax.rem(me + step, DEPTH)
        pltpu.make_async_remote_copy(
            src_ref=parts.at[src], dst_ref=got.at[src], send_sem=send_sem.at[src], recv_sem=recv_sem.at[src],
            device_id={"depth": src}, device_id_type=MESH,
        ).wait_recv()

    through = got[0, 0]
    w_sum, r_sum, g_sum = got[0, 1], got[0, 2], got[0, 3]
    for i in range(1, DEPTH):
        w_sum += through * got[i, 1]
        r_sum += through * got[i, 2]
        g_sum += through * got[i, 3]
        through = through * got[i, 0]
    out_ref[0] = (w_sum + r_sum) * (0.5 * SCALE)
    out_ref[1] = g_sum * SCALE
    out_ref[2] = (w_sum - r_sum) * (0.5 * SCALE)
    out_ref[3] = 1.0 - through

    for step in range(1, DEPTH):
        send(lax.rem(me + step, DEPTH)).wait_send()
    for has, copy in ((down, x_up), (up, x_dn)):
        pl.when(has)(copy.wait_send)

    def sent_edges(b, _):
        for copies, to_high, to_low in ((z_copies(b), back, front), (y_copies(b), right, left)):
            pl.when(to_high)(copies[0].wait_send)
            pl.when(to_low)(copies[1].wait_send)
        return 0

    lax.fori_loop(0, DEPTH, sent_edges, 0)


def on_device(density):
    vmem, dma = pl.BlockSpec(memory_space=pltpu.VMEM), pltpu.SemaphoreType.DMA
    return pl.pallas_call(
        kernel,
        out_shape=jax.ShapeDtypeStruct((4, ROWS, Y), F32),
        in_specs=[pl.BlockSpec(memory_space=pl.ANY)],
        out_specs=vmem,
        scratch_shapes=[
            pltpu.VMEM((Y + 256, Y), BF16),
            pltpu.VMEM((6 * ROWS, 256), BF16),
            pltpu.VMEM((2, 16, 128), BF16),
            pltpu.VMEM((2, 128, 16), BF16),
            pltpu.VMEM((Z + 4, X + 2 * EDGE, Y), BF16),
            pltpu.VMEM((2, DEPTH, ROWS, 128), BF16),
            pltpu.VMEM((2, DEPTH, ROWS, 128), BF16),
            pltpu.VMEM((2, 2 * Z, Y), BF16),
            pltpu.VMEM((2, 2 * Z, Y), BF16),
            pltpu.VMEM((DEPTH, 4, ROWS, Y), F32),
            pltpu.VMEM((DEPTH, 4, ROWS, Y), F32),
        ]
        + [dma((DEPTH,))]
        + [dma((2, DEPTH))] * 2
        + [dma((2,))] * 2
        + [dma((2, DEPTH))] * 2
        + [dma((DEPTH,))] * 2
        + [pltpu.VMEM((8, ROWS, Y), F32)] * 4
        + [pltpu.VMEM((3, 8, ROWS, Y), F32)] * 4,
        compiler_params=pltpu.CompilerParams(collective_id=0, has_side_effects=True, vmem_limit_bytes=48 << 20),
        name="render",
    )(density)


def solution(mesh):
    return jax.shard_map(
        on_device,
        mesh=mesh,
        in_specs=(P("depth", "ix", "iy"),),
        out_specs=P(None, ("ix", "depth"), "iy"),
        check_vma=False,
    )
```

```python
import jax
import jax.numpy as jnp
import numpy as np
from jax import lax
from jax.experimental import pallas as pl
from jax.experimental.pallas import tpu as pltpu
from jax.sharding import PartitionSpec as P

MESH = pl.DeviceIdType.MESH
F32, BF16 = jnp.float32, jnp.bfloat16
Z, X, Y = 64, 256, 256
DEPTH = 8
ROWS = X // DEPTH
EDGE = 16
NZ = 512
LAG = 3
EXP2_2D = float(2.0 * np.log2(np.e))
EXP2_K = float(-0.1 * np.log2(np.e) / NZ)
EXP2_SQ = float(-np.log2(np.e))
SCALE = 0.7 * 16.0 / 25.0
BASE = 0.3 / SCALE


def tap(step):
    near = jnp.where(step == 1, 8.0, jnp.where(step == -1, -8.0, 0.0))
    return jnp.where(step == 2, -1.0, jnp.where(step == -2, 1.0, near))


def fill_matrices(y_mat, zx_mat, pick, spread):
    k, y = (lax.broadcasted_iota(jnp.int32, (256, Y), i) for i in (0, 1))
    y_mat[:256] = tap(k - y).astype(BF16)
    low = (k & 64) == ((k & 128) >> 1)
    y_mat[256:] = tap(jnp.where(low, (k & 1) - 2, Y + (k & 1)) - y).astype(BF16)
    m, c = (lax.broadcasted_iota(jnp.int32, (2 * ROWS, 256), i) for i in (0, 1))
    layer, row = m >> 5, m & 31
    at = jnp.where(c < 64, c >> 5, jnp.where(c < 192, 1 + (c >> 6), (c >> 5) - 2))
    across = jnp.where((c >= 64) & (c < 192), (c & 63) - EDGE, c & 31)
    gx = jnp.where(at == layer + 2, tap(across - row), 0.0)
    gz = jnp.where(across == row, tap(at - 2 - layer), 0.0)
    for i, g in enumerate((gx, gz, (15.0 / 16.0) * gx + (12.0 / 16.0) * gz)):
        zx_mat[2 * ROWS * i : 2 * ROWS * (i + 1)] = g.astype(BF16)
    m, c = (lax.broadcasted_iota(jnp.int32, (16, 128), i) for i in (0, 1))
    o, q = (lax.broadcasted_iota(jnp.int32, (128, 16), i) for i in (0, 1))
    for side, start in ((0, 0), (1, 14)):
        pick[side] = jnp.where(((c >> 4) == (m >> 1)) & ((c & 15) == start + (m & 1)), 1.0, 0.0).astype(BF16)
        spread[1 - side] = jnp.where(((o >> 4) == (q >> 1)) & ((o & 15) == start + (q & 1)), 1.0, 0.0).astype(BF16)


def kernel(
    x_ref, out_ref,
    y_mat, zx_mat, pick, spread, cells, halo, pack, row_pack, row_halo, parts, got,
    load_sem, z_send, z_recv, x_send, x_recv, y_send, y_recv, send_sem, recv_sem, *slopes,
):
    me = lax.axis_index("depth")
    ix, iy = lax.axis_index("ix"), lax.axis_index("iy")
    n_ix, n_iy = lax.axis_size("ix"), lax.axis_size("iy")
    front, back = me > 0, me < DEPTH - 1
    up, down = ix > 0, ix < n_ix - 1
    left, right = iy > 0, iy < n_iy - 1

    def block(i, at=me):
        swapped = jnp.where(jnp.logical_and(jnp.logical_or(at == 0, at == DEPTH - 1), i < 2), 1 - i, i)
        return lax.rem(jnp.where((at & 1) == 1, at + 1 + swapped, at + 2 * DEPTH - 1 - swapped), DEPTH)

    def load(b):
        rows = pl.ds(pl.multiple_of(ROWS * b, ROWS), ROWS)
        inner = pl.ds(pl.multiple_of(EDGE + ROWS * b, EDGE), ROWS)
        return pltpu.make_async_copy(x_ref.at[:, rows], cells.at[pl.ds(2, Z), inner], load_sem.at[b])

    barrier = pltpu.get_barrier_semaphore()
    for step in range(1, DEPTH):
        pl.semaphore_signal(barrier, inc=1, device_id={"depth": lax.rem(me + step, DEPTH)}, device_id_type=MESH)
    for axis, at, count in (("ix", ix, n_ix), ("iy", iy, n_iy)):
        for step in (1, count - 1):
            pl.semaphore_signal(barrier, inc=1, device_id={axis: lax.rem(at + step, count)}, device_id_type=MESH)
    for i in range(DEPTH):
        load(block(i)).start()

    def remote(src, dst, sems, recvs, k, axis, to):
        return pltpu.make_async_remote_copy(
            src_ref=src, dst_ref=dst, send_sem=sems.at[k], recv_sem=recvs.at[k],
            device_id={axis: to}, device_id_type=MESH,
        )

    def z_copies(b):
        rows = pl.ds(pl.multiple_of(ROWS * b, ROWS), ROWS)
        inner = pl.ds(pl.multiple_of(EDGE + ROWS * b, EDGE), ROWS)
        low = pltpu.make_async_remote_copy(
            src_ref=x_ref.at[pl.ds(Z - 2, 2), rows], dst_ref=cells.at[pl.ds(0, 2), inner], send_sem=z_send.at[0, b], recv_sem=z_recv.at[0, b],
            device_id={"depth": lax.rem(me + 1, DEPTH)}, device_id_type=MESH,
        )
        high = pltpu.make_async_remote_copy(
            src_ref=x_ref.at[pl.ds(0, 2), rows], dst_ref=cells.at[pl.ds(Z + 2, 2), inner], send_sem=z_send.at[1, b], recv_sem=z_recv.at[1, b],
            device_id={"depth": lax.rem(me + DEPTH - 1, DEPTH)}, device_id_type=MESH,
        )
        return low, high

    x_up = remote(row_pack.at[1], row_halo.at[0], x_send, x_recv, 0, "ix", lax.rem(ix + 1, n_ix))
    x_dn = remote(row_pack.at[0], row_halo.at[1], x_send, x_recv, 1, "ix", lax.rem(ix + n_ix - 1, n_ix))

    def y_copies(b):
        low = pltpu.make_async_remote_copy(
            src_ref=pack.at[1, b], dst_ref=halo.at[0, b], send_sem=y_send.at[0, b], recv_sem=y_recv.at[0, b],
            device_id={"iy": lax.rem(iy + 1, n_iy)}, device_id_type=MESH,
        )
        high = pltpu.make_async_remote_copy(
            src_ref=pack.at[0, b], dst_ref=halo.at[1, b], send_sem=y_send.at[1, b], recv_sem=y_recv.at[1, b],
            device_id={"iy": lax.rem(iy + n_iy - 1, n_iy)}, device_id_type=MESH,
        )
        return low, high


    @pl.when(jnp.logical_not(front))
    def _():
        cells[0:2] = jnp.zeros((2,) + cells.shape[1:], BF16)

    @pl.when(jnp.logical_not(back))
    def _():
        cells[Z + 2 : Z + 4] = jnp.zeros((2,) + cells.shape[1:], BF16)


    fill_matrices(y_mat, zx_mat, pick, spread)
    for side, has in ((0, left), (1, right)):

        @pl.when(jnp.logical_not(has))
        def _(side=side):
            halo[side] = jnp.zeros(halo.shape[1:], BF16)

    for side, has in ((0, up), (1, down)):

        @pl.when(jnp.logical_not(has))
        def _(side=side):
            row_halo[side] = jnp.zeros(row_halo.shape[1:], BF16)

    lane = lax.broadcasted_iota(jnp.int32, (16, 128), 1)

    def pack_columns(b, half):
        rows = pl.ds(pl.multiple_of(EDGE + ROWS * b + 16 * half, EDGE), 16)
        first, last = jnp.zeros((16, 128), F32), jnp.zeros((16, 128), F32)
        for z in range(Z):
            ends = jnp.where(lane < 2, cells[2 + z, rows, :128].astype(F32), cells[2 + z, rows, Y - 128 :].astype(F32))
            moved = pltpu.roll(ends, 2 * z, axis=1) if z else ends
            first = jnp.where(lane >> 1 == z, moved, first)
            last = jnp.where(lane >> 1 == (z + 63) & 63, moved, last)
        last = pltpu.roll(last, 2, axis=1)
        first = pltpu.roll(first, 64, axis=1)
        at = pl.ds(pl.multiple_of(16 * half, 16), 16)
        pack[0, b, at] = first.astype(BF16)
        pack[1, b, at] = last.astype(BF16)

    def pack_block(i, _):
        b = block(i)
        load(b).wait()

        def one(half, _):
            pack_columns(b, half)
            return 0

        lax.fori_loop(0, 2, one, 0)
        return 0

    lax.fori_loop(0, DEPTH, pack_block, 0)
    for side, row in ((0, EDGE), (1, X)):
        for c in range(Z // 8):
            tiles = cells[2 + 8 * c : 10 + 8 * c, row : row + 16].reshape(128, Y)
            picked = jnp.dot(pick[side], tiles, preferred_element_type=F32)
            row_pack[side, 16 * c : 16 * c + 16] = picked.astype(BF16)

    slots = tuple(zip(slopes[:4], slopes[4:]))

    def place(n):
        return block(n >> 3), n & 7

    def slopes_y(n, first):
        b, c = place(n)
        inner = pl.ds(pl.multiple_of(EDGE + ROWS * b, EDGE), ROWS)
        lanes = lax.broadcasted_iota(jnp.int32, (ROWS, 128), 1)
        late = c >> 2
        sides = jnp.where(lanes < 64, halo[late, b], halo[1 - late, b])
        layer_of = ((lanes & 63) >> 1) + 32 * late
        outer = jnp.stack([jnp.where(layer_of == 8 * c + i, sides, jnp.zeros_like(sides)) for i in range(16)])
        tiles = cells[pl.ds(2 + 8 * c, 16), inner].reshape(16 * ROWS, Y)
        gy = jnp.dot(tiles, y_mat[:Y], preferred_element_type=F32)
        gy += jnp.dot(outer.reshape(16 * ROWS, 128), y_mat[pl.ds(pl.multiple_of(Y + 128 * late, 128), 128)], preferred_element_type=F32)
        gy = gy.reshape(2, 8, ROWS, Y)
        slots[first][0][...] = gy[0]
        slots[first + 1][0][...] = gy[1]

    def slopes_zx(n, slot, j):
        b, c = place(n)
        z = 8 * c + 2 * j
        wide = pl.ds(pl.multiple_of(ROWS * b, ROWS), ROWS + 2 * EDGE)
        inner = pl.ds(pl.multiple_of(EDGE + ROWS * b, EDGE), ROWS)
        tiles = [cells[z, inner], cells[z + 1, inner], cells[z + 2, wide], cells[z + 3, wide], cells[z + 4, inner], cells[z + 5, inner]]
        g = jnp.dot(zx_mat[...], jnp.concatenate(tiles, axis=0), preferred_element_type=F32)
        slots[slot][1][:, 2 * j : 2 * j + 2] = g.reshape(3, 2, ROWS, Y)

    for j in range(1, 8):
        slopes_zx(j // 4, j // 4, j % 4)

    pl.semaphore_wait(barrier, DEPTH - 1 + 4)

    def send_layers(i, _):
        pl.when(back)(z_copies(block(i, me + 1))[0].start)
        pl.when(front)(z_copies(block(i, me - 1))[1].start)
        return 0

    def send_columns(i, _):
        low, high = y_copies(block(i))
        pl.when(right)(low.start)
        pl.when(left)(high.start)
        return 0

    send_columns(0, 0)
    send_layers(0, 0)
    pl.when(down)(x_up.start)
    pl.when(up)(x_dn.start)

    def send_rest(i, _):
        send_columns(i, 0)
        return send_layers(i, 0)

    lax.fori_loop(1, DEPTH, send_rest, 0)

    def wait_front(b):
        low, high = y_copies(b)
        pl.when(left)(low.wait_recv)
        pl.when(right)(high.wait_recv)
        pl.when(front)(z_copies(b)[0].wait_recv)
        for side, has, copy, at, row in ((0, up, x_up, 0, 0), (1, down, x_dn, DEPTH - 1, X + EDGE)):

            @pl.when(b == at)
            def _(side=side, has=has, copy=copy, row=row):
                pl.when(has)(copy.wait_recv)
                for c in range(Z // 8):
                    tiles = jnp.dot(spread[side], row_halo[side, 16 * c : 16 * c + 16], preferred_element_type=F32)
                    cells[2 + 8 * c : 10 + 8 * c, row : row + 16] = tiles.astype(BF16).reshape(8, 16, Y)

    def wait_back(b):
        pl.when(back)(z_copies(b)[1].wait_recv)

    wait_front(block(0))

    def march(n, slot, s, after):
        b, c = place(n)
        gy_ref, g_ref = slots[slot]
        row, lane = (s // 2) * 16, (s % 2) * 128
        rs, ls = slice(row, row + 16), slice(lane, lane + 128)
        inner = pl.ds(pl.multiple_of(EDGE + ROWS * b + row, EDGE), 16)
        t, w_sum, r_sum, g_sum = (parts[b, k, rs, ls] for k in range(4))
        for ref in after:
            t = t + 0.0 * ref[rs, ls]
        for i in range(8):
            d = cells[2 + 8 * c + i, inner, ls].astype(F32)
            gx, gz, gy = g_ref[0, i, rs, ls], g_ref[1, i, rs, ls], gy_ref[i, rs, ls]
            along = g_ref[2, i, rs, ls] + gy
            n2 = gx * gx + gz * gz + (gy * gy + 144.0)
            bright = jnp.abs(along) * lax.rsqrt(n2) + BASE
            grow = jnp.exp2(d * EXP2_2D)
            k5 = grow + pltpu.reciprocal(grow, approx=True)
            t_next = t * jnp.exp2(k5 * EXP2_K)
            w = (t - t_next) * bright
            t = t_next
            w_sum = w_sum + w
            r_sum = r_sum + w * jnp.tanh(d)
            g_sum = g_sum + w * jnp.exp2(d * (d * EXP2_SQ))
        for k, v in enumerate((t, w_sum, r_sum, g_sum)):
            parts[b, k, rs, ls] = v

    def send(b):
        return pltpu.make_async_remote_copy(
            src_ref=parts.at[b], dst_ref=got.at[me], send_sem=send_sem.at[b], recv_sem=recv_sem.at[me],
            device_id={"depth": b}, device_id_type=MESH,
        )

    slopes_zx(0, 0, 0)
    slopes_y(0, 0)

    def turn(m, _):
        i, quarter = m >> 2, m & 3
        b = block(i)

        @pl.when(quarter == 0)
        def _():
            parts[b, 0] = jnp.ones((ROWS, Y), F32)
            for p in (1, 2, 3):
                parts[b, p] = jnp.zeros((ROWS, Y), F32)

        pl.when(quarter == 2)(lambda: wait_back(b))
        pl.when(jnp.logical_and(quarter == 3, i < DEPTH - 1))(lambda: wait_front(block(i + 1)))

        for h in range(2):

            @pl.when((m & 1) == h)
            def _(h=h):
                use, fill = 2 * h, 2 - 2 * h
                slopes_y(2 * m + 2, fill)
                for p in range(8):
                    slopes_zx(2 * m + 2 + p // 4, fill + p // 4, p % 4)
                    after = [slots[fill + (p - LAG) // 4][1].at[0, 2 * ((p - LAG) % 4)]] if p >= LAG else []
                    if p in (5, 6):
                        after.append(slots[fill + (p == 6)][0].at[7])
                    march(2 * m + p % 2, use + p % 2, p // 2, after)

        @pl.when(jnp.logical_and(quarter == 3, i < DEPTH - 1))
        def _():
            send(b).start()

        return 0

    lax.fori_loop(0, 4 * DEPTH, turn, 0)

    got[me] = parts[me]
    for step in range(1, DEPTH):
        src = lax.rem(me + step, DEPTH)
        pltpu.make_async_remote_copy(
            src_ref=parts.at[src], dst_ref=got.at[src], send_sem=send_sem.at[src], recv_sem=recv_sem.at[src],
            device_id={"depth": src}, device_id_type=MESH,
        ).wait_recv()

    through = got[0, 0]
    w_sum, r_sum, g_sum = got[0, 1], got[0, 2], got[0, 3]
    for i in range(1, DEPTH):
        w_sum += through * got[i, 1]
        r_sum += through * got[i, 2]
        g_sum += through * got[i, 3]
        through = through * got[i, 0]
    out_ref[0] = (w_sum + r_sum) * (0.5 * SCALE)
    out_ref[1] = g_sum * SCALE
    out_ref[2] = (w_sum - r_sum) * (0.5 * SCALE)
    out_ref[3] = 1.0 - through

    for step in range(1, DEPTH):
        send(lax.rem(me + step, DEPTH)).wait_send()
    for has, copy in ((down, x_up), (up, x_dn)):
        pl.when(has)(copy.wait_send)

    def sent_edges(b, _):
        for copies, to_high, to_low in ((z_copies(b), back, front), (y_copies(b), right, left)):
            pl.when(to_high)(copies[0].wait_send)
            pl.when(to_low)(copies[1].wait_send)
        return 0

    lax.fori_loop(0, DEPTH, sent_edges, 0)


def on_device(density):
    vmem, dma = pl.BlockSpec(memory_space=pltpu.VMEM), pltpu.SemaphoreType.DMA
    return pl.pallas_call(
        kernel,
        out_shape=jax.ShapeDtypeStruct((4, ROWS, Y), F32),
        in_specs=[pl.BlockSpec(memory_space=pl.ANY)],
        out_specs=vmem,
        scratch_shapes=[
            pltpu.VMEM((Y + 256, Y), BF16),
            pltpu.VMEM((6 * ROWS, 256), BF16),
            pltpu.VMEM((2, 16, 128), BF16),
            pltpu.VMEM((2, 128, 16), BF16),
            pltpu.VMEM((Z + 4, X + 2 * EDGE, Y), BF16),
            pltpu.VMEM((2, DEPTH, ROWS, 128), BF16),
            pltpu.VMEM((2, DEPTH, ROWS, 128), BF16),
            pltpu.VMEM((2, 2 * Z, Y), BF16),
            pltpu.VMEM((2, 2 * Z, Y), BF16),
            pltpu.VMEM((DEPTH, 4, ROWS, Y), F32),
            pltpu.VMEM((DEPTH, 4, ROWS, Y), F32),
        ]
        + [dma((DEPTH,))]
        + [dma((2, DEPTH))] * 2
        + [dma((2,))] * 2
        + [dma((2, DEPTH))] * 2
        + [dma((DEPTH,))] * 2
        + [pltpu.VMEM((8, ROWS, Y), F32)] * 4
        + [pltpu.VMEM((3, 8, ROWS, Y), F32)] * 4,
        compiler_params=pltpu.CompilerParams(collective_id=0, has_side_effects=True, vmem_limit_bytes=48 << 20),
        name="render",
    )(density)


def solution(mesh):
    return jax.shard_map(
        on_device,
        mesh=mesh,
        in_specs=(P("depth", "ix", "iy"),),
        out_specs=P(None, ("ix", "depth"), "iy"),
        check_vma=False,
    )
```

```python
import jax
import jax.numpy as jnp
import numpy as np
from jax import lax
from jax.experimental import pallas as pl
from jax.experimental.pallas import tpu as pltpu
from jax.sharding import PartitionSpec as P

MESH = pl.DeviceIdType.MESH
F32, BF16 = jnp.float32, jnp.bfloat16
Z, X, Y = 64, 256, 256
DEPTH = 8
ROWS = X // DEPTH
EDGE = 16
NZ = 512
LAG = 2
EXP2_2D = float(2.0 * np.log2(np.e))
EXP2_K = float(-0.1 * np.log2(np.e) / NZ)
EXP2_SQ = float(-np.log2(np.e))
SCALE = 0.7 * 16.0 / 25.0
BASE = 0.3 / SCALE


def tap(step):
    near = jnp.where(step == 1, 8.0, jnp.where(step == -1, -8.0, 0.0))
    return jnp.where(step == 2, -1.0, jnp.where(step == -2, 1.0, near))


def fill_matrices(y_mat, zx_mat, pick, spread):
    k, y = (lax.broadcasted_iota(jnp.int32, (256, Y), i) for i in (0, 1))
    y_mat[:256] = tap(k - y).astype(BF16)
    low = (k & 64) == ((k & 128) >> 1)
    y_mat[256:] = tap(jnp.where(low, (k & 1) - 2, Y + (k & 1)) - y).astype(BF16)
    m, c = (lax.broadcasted_iota(jnp.int32, (2 * ROWS, 256), i) for i in (0, 1))
    layer, row = m >> 5, m & 31
    at = jnp.where(c < 64, c >> 5, jnp.where(c < 192, 1 + (c >> 6), (c >> 5) - 2))
    across = jnp.where((c >= 64) & (c < 192), (c & 63) - EDGE, c & 31)
    gx = jnp.where(at == layer + 2, tap(across - row), 0.0)
    gz = jnp.where(across == row, tap(at - 2 - layer), 0.0)
    for i, g in enumerate((gx, gz, (15.0 / 16.0) * gx + (12.0 / 16.0) * gz)):
        zx_mat[2 * ROWS * i : 2 * ROWS * (i + 1)] = g.astype(BF16)
    m, c = (lax.broadcasted_iota(jnp.int32, (16, 128), i) for i in (0, 1))
    o, q = (lax.broadcasted_iota(jnp.int32, (128, 16), i) for i in (0, 1))
    for side, start in ((0, 0), (1, 14)):
        pick[side] = jnp.where(((c >> 4) == (m >> 1)) & ((c & 15) == start + (m & 1)), 1.0, 0.0).astype(BF16)
        spread[1 - side] = jnp.where(((o >> 4) == (q >> 1)) & ((o & 15) == start + (q & 1)), 1.0, 0.0).astype(BF16)


def kernel(
    x_ref, out_ref,
    y_mat, zx_mat, pick, spread, cells, halo, pack, row_pack, row_halo, parts, got,
    load_sem, z_send, z_recv, x_send, x_recv, y_send, y_recv, send_sem, recv_sem, *slopes,
):
    me = lax.axis_index("depth")
    ix, iy = lax.axis_index("ix"), lax.axis_index("iy")
    n_ix, n_iy = lax.axis_size("ix"), lax.axis_size("iy")
    front, back = me > 0, me < DEPTH - 1
    up, down = ix > 0, ix < n_ix - 1
    left, right = iy > 0, iy < n_iy - 1

    def block(i, at=me):
        swapped = jnp.where(jnp.logical_and(jnp.logical_or(at == 0, at == DEPTH - 1), i < 2), 1 - i, i)
        return lax.rem(jnp.where((at & 1) == 1, at + 1 + swapped, at + 2 * DEPTH - 1 - swapped), DEPTH)

    def load(b):
        rows = pl.ds(pl.multiple_of(ROWS * b, ROWS), ROWS)
        inner = pl.ds(pl.multiple_of(EDGE + ROWS * b, EDGE), ROWS)
        return pltpu.make_async_copy(x_ref.at[:, rows], cells.at[pl.ds(2, Z), inner], load_sem.at[b])

    barrier = pltpu.get_barrier_semaphore()
    for step in range(1, DEPTH):
        pl.semaphore_signal(barrier, inc=1, device_id={"depth": lax.rem(me + step, DEPTH)}, device_id_type=MESH)
    for axis, at, count in (("ix", ix, n_ix), ("iy", iy, n_iy)):
        for step in (1, count - 1):
            pl.semaphore_signal(barrier, inc=1, device_id={axis: lax.rem(at + step, count)}, device_id_type=MESH)
    for i in range(DEPTH):
        load(block(i)).start()

    def remote(src, dst, sems, recvs, k, axis, to):
        return pltpu.make_async_remote_copy(
            src_ref=src, dst_ref=dst, send_sem=sems.at[k], recv_sem=recvs.at[k],
            device_id={axis: to}, device_id_type=MESH,
        )

    def z_copies(b):
        rows = pl.ds(pl.multiple_of(ROWS * b, ROWS), ROWS)
        inner = pl.ds(pl.multiple_of(EDGE + ROWS * b, EDGE), ROWS)
        low = pltpu.make_async_remote_copy(
            src_ref=x_ref.at[pl.ds(Z - 2, 2), rows], dst_ref=cells.at[pl.ds(0, 2), inner], send_sem=z_send.at[0, b], recv_sem=z_recv.at[0, b],
            device_id={"depth": lax.rem(me + 1, DEPTH)}, device_id_type=MESH,
        )
        high = pltpu.make_async_remote_copy(
            src_ref=x_ref.at[pl.ds(0, 2), rows], dst_ref=cells.at[pl.ds(Z + 2, 2), inner], send_sem=z_send.at[1, b], recv_sem=z_recv.at[1, b],
            device_id={"depth": lax.rem(me + DEPTH - 1, DEPTH)}, device_id_type=MESH,
        )
        return low, high

    x_up = remote(row_pack.at[1], row_halo.at[0], x_send, x_recv, 0, "ix", lax.rem(ix + 1, n_ix))
    x_dn = remote(row_pack.at[0], row_halo.at[1], x_send, x_recv, 1, "ix", lax.rem(ix + n_ix - 1, n_ix))

    def y_copies(b):
        low = pltpu.make_async_remote_copy(
            src_ref=pack.at[1, b], dst_ref=halo.at[0, b], send_sem=y_send.at[0, b], recv_sem=y_recv.at[0, b],
            device_id={"iy": lax.rem(iy + 1, n_iy)}, device_id_type=MESH,
        )
        high = pltpu.make_async_remote_copy(
            src_ref=pack.at[0, b], dst_ref=halo.at[1, b], send_sem=y_send.at[1, b], recv_sem=y_recv.at[1, b],
            device_id={"iy": lax.rem(iy + n_iy - 1, n_iy)}, device_id_type=MESH,
        )
        return low, high


    @pl.when(jnp.logical_not(front))
    def _():
        cells[0:2] = jnp.zeros((2,) + cells.shape[1:], BF16)

    @pl.when(jnp.logical_not(back))
    def _():
        cells[Z + 2 : Z + 4] = jnp.zeros((2,) + cells.shape[1:], BF16)


    fill_matrices(y_mat, zx_mat, pick, spread)
    for side, has in ((0, left), (1, right)):

        @pl.when(jnp.logical_not(has))
        def _(side=side):
            halo[side] = jnp.zeros(halo.shape[1:], BF16)

    for side, has in ((0, up), (1, down)):

        @pl.when(jnp.logical_not(has))
        def _(side=side):
            row_halo[side] = jnp.zeros(row_halo.shape[1:], BF16)

    lane = lax.broadcasted_iota(jnp.int32, (16, 128), 1)

    def pack_columns(b, half):
        rows = pl.ds(pl.multiple_of(EDGE + ROWS * b + 16 * half, EDGE), 16)
        first, last = jnp.zeros((16, 128), F32), jnp.zeros((16, 128), F32)
        for z in range(Z):
            ends = jnp.where(lane < 2, cells[2 + z, rows, :128].astype(F32), cells[2 + z, rows, Y - 128 :].astype(F32))
            moved = pltpu.roll(ends, 2 * z, axis=1) if z else ends
            first = jnp.where(lane >> 1 == z, moved, first)
            last = jnp.where(lane >> 1 == (z + 63) & 63, moved, last)
        last = pltpu.roll(last, 2, axis=1)
        first = pltpu.roll(first, 64, axis=1)
        at = pl.ds(pl.multiple_of(16 * half, 16), 16)
        pack[0, b, at] = first.astype(BF16)
        pack[1, b, at] = last.astype(BF16)

    def pack_block(i, _):
        b = block(i)
        load(b).wait()

        def one(half, _):
            pack_columns(b, half)
            return 0

        lax.fori_loop(0, 2, one, 0)
        return 0

    lax.fori_loop(0, DEPTH, pack_block, 0)
    for side, row in ((0, EDGE), (1, X)):
        for c in range(Z // 8):
            tiles = cells[2 + 8 * c : 10 + 8 * c, row : row + 16].reshape(128, Y)
            picked = jnp.dot(pick[side], tiles, preferred_element_type=F32)
            row_pack[side, 16 * c : 16 * c + 16] = picked.astype(BF16)

    slots = tuple(zip(slopes[:4], slopes[4:]))

    def place(n):
        return block(n >> 3), n & 7

    def slopes_y(n, first):
        b, c = place(n)
        inner = pl.ds(pl.multiple_of(EDGE + ROWS * b, EDGE), ROWS)
        lanes = lax.broadcasted_iota(jnp.int32, (ROWS, 128), 1)
        late = c >> 2
        sides = jnp.where(lanes < 64, halo[late, b], halo[1 - late, b])
        layer_of = ((lanes & 63) >> 1) + 32 * late
        outer = jnp.stack([jnp.where(layer_of == 8 * c + i, sides, jnp.zeros_like(sides)) for i in range(16)])
        tiles = cells[pl.ds(2 + 8 * c, 16), inner].reshape(16 * ROWS, Y)
        gy = jnp.dot(tiles, y_mat[:Y], preferred_element_type=F32)
        gy += jnp.dot(outer.reshape(16 * ROWS, 128), y_mat[pl.ds(pl.multiple_of(Y + 128 * late, 128), 128)], preferred_element_type=F32)
        gy = gy.reshape(2, 8, ROWS, Y)
        slots[first][0][...] = gy[0]
        slots[first + 1][0][...] = gy[1]

    def slopes_zx(n, slot, j):
        b, c = place(n)
        z = 8 * c + 2 * j
        wide = pl.ds(pl.multiple_of(ROWS * b, ROWS), ROWS + 2 * EDGE)
        inner = pl.ds(pl.multiple_of(EDGE + ROWS * b, EDGE), ROWS)
        tiles = [cells[z, inner], cells[z + 1, inner], cells[z + 2, wide], cells[z + 3, wide], cells[z + 4, inner], cells[z + 5, inner]]
        g = jnp.dot(zx_mat[...], jnp.concatenate(tiles, axis=0), preferred_element_type=F32)
        slots[slot][1][:, 2 * j : 2 * j + 2] = g.reshape(3, 2, ROWS, Y)

    for j in range(1, 8):
        slopes_zx(j // 4, j // 4, j % 4)

    pl.semaphore_wait(barrier, DEPTH - 1 + 4)

    def send_layers(i, _):
        pl.when(back)(z_copies(block(i, me + 1))[0].start)
        pl.when(front)(z_copies(block(i, me - 1))[1].start)
        return 0

    def send_columns(i, _):
        low, high = y_copies(block(i))
        pl.when(right)(low.start)
        pl.when(left)(high.start)
        return 0

    send_columns(0, 0)
    send_layers(0, 0)
    pl.when(down)(x_up.start)
    pl.when(up)(x_dn.start)

    def send_rest(i, _):
        send_columns(i, 0)
        return send_layers(i, 0)

    lax.fori_loop(1, DEPTH, send_rest, 0)

    def wait_front(b):
        low, high = y_copies(b)
        pl.when(left)(low.wait_recv)
        pl.when(right)(high.wait_recv)
        pl.when(front)(z_copies(b)[0].wait_recv)
        for side, has, copy, at, row in ((0, up, x_up, 0, 0), (1, down, x_dn, DEPTH - 1, X + EDGE)):

            @pl.when(b == at)
            def _(side=side, has=has, copy=copy, row=row):
                pl.when(has)(copy.wait_recv)
                for c in range(Z // 8):
                    tiles = jnp.dot(spread[side], row_halo[side, 16 * c : 16 * c + 16], preferred_element_type=F32)
                    cells[2 + 8 * c : 10 + 8 * c, row : row + 16] = tiles.astype(BF16).reshape(8, 16, Y)

    def wait_back(b):
        pl.when(back)(z_copies(b)[1].wait_recv)

    wait_front(block(0))

    def march(n, slot, s, after):
        b, c = place(n)
        gy_ref, g_ref = slots[slot]
        row, lane = (s // 2) * 16, (s % 2) * 128
        rs, ls = slice(row, row + 16), slice(lane, lane + 128)
        inner = pl.ds(pl.multiple_of(EDGE + ROWS * b + row, EDGE), 16)
        t, w_sum, r_sum, g_sum = (parts[b, k, rs, ls] for k in range(4))
        for ref in after:
            t = t + 0.0 * ref[rs, ls]
        for i in range(8):
            d = cells[2 + 8 * c + i, inner, ls].astype(F32)
            gx, gz, gy = g_ref[0, i, rs, ls], g_ref[1, i, rs, ls], gy_ref[i, rs, ls]
            along = g_ref[2, i, rs, ls] + gy
            n2 = gx * gx + gz * gz + (gy * gy + 144.0)
            bright = jnp.abs(along) * lax.rsqrt(n2) + BASE
            grow = jnp.exp2(d * EXP2_2D)
            k5 = grow + pltpu.reciprocal(grow, approx=True)
            t_next = t * jnp.exp2(k5 * EXP2_K)
            w = (t - t_next) * bright
            t = t_next
            w_sum = w_sum + w
            r_sum = r_sum + w * jnp.tanh(d)
            g_sum = g_sum + w * jnp.exp2(d * (d * EXP2_SQ))
        for k, v in enumerate((t, w_sum, r_sum, g_sum)):
            parts[b, k, rs, ls] = v

    def send(b):
        return pltpu.make_async_remote_copy(
            src_ref=parts.at[b], dst_ref=got.at[me], send_sem=send_sem.at[b], recv_sem=recv_sem.at[me],
            device_id={"depth": b}, device_id_type=MESH,
        )

    slopes_zx(0, 0, 0)
    slopes_y(0, 0)

    def turn(m, _):
        i, quarter = m >> 2, m & 3
        b = block(i)

        @pl.when(quarter == 0)
        def _():
            parts[b, 0] = jnp.ones((ROWS, Y), F32)
            for p in (1, 2, 3):
                parts[b, p] = jnp.zeros((ROWS, Y), F32)

        pl.when(quarter == 2)(lambda: wait_back(b))
        pl.when(jnp.logical_and(quarter == 3, i < DEPTH - 1))(lambda: wait_front(block(i + 1)))

        for h in range(2):

            @pl.when((m & 1) == h)
            def _(h=h):
                use, fill = 2 * h, 2 - 2 * h
                slopes_y(2 * m + 2, fill)
                for p in range(8):
                    slopes_zx(2 * m + 2 + p // 4, fill + p // 4, p % 4)
                    after = [slots[fill + (p - LAG) // 4][1].at[0, 2 * ((p - LAG) % 4)]] if p >= LAG else []
                    if p in (5, 6):
                        after.append(slots[fill + (p == 6)][0].at[7])
                    march(2 * m + p % 2, use + p % 2, p // 2, after)

        @pl.when(jnp.logical_and(quarter == 3, i < DEPTH - 1))
        def _():
            send(b).start()

        return 0

    lax.fori_loop(0, 4 * DEPTH, turn, 0)

    got[me] = parts[me]
    for step in range(1, DEPTH):
        src = lax.rem(me + step, DEPTH)
        pltpu.make_async_remote_copy(
            src_ref=parts.at[src], dst_ref=got.at[src], send_sem=send_sem.at[src], recv_sem=recv_sem.at[src],
            device_id={"depth": src}, device_id_type=MESH,
        ).wait_recv()

    through = got[0, 0]
    w_sum, r_sum, g_sum = got[0, 1], got[0, 2], got[0, 3]
    for i in range(1, DEPTH):
        w_sum += through * got[i, 1]
        r_sum += through * got[i, 2]
        g_sum += through * got[i, 3]
        through = through * got[i, 0]
    out_ref[0] = (w_sum + r_sum) * (0.5 * SCALE)
    out_ref[1] = g_sum * SCALE
    out_ref[2] = (w_sum - r_sum) * (0.5 * SCALE)
    out_ref[3] = 1.0 - through

    for step in range(1, DEPTH):
        send(lax.rem(me + step, DEPTH)).wait_send()
    for has, copy in ((down, x_up), (up, x_dn)):
        pl.when(has)(copy.wait_send)

    def sent_edges(b, _):
        for copies, to_high, to_low in ((z_copies(b), back, front), (y_copies(b), right, left)):
            pl.when(to_high)(copies[0].wait_send)
            pl.when(to_low)(copies[1].wait_send)
        return 0

    lax.fori_loop(0, DEPTH, sent_edges, 0)


def on_device(density):
    vmem, dma = pl.BlockSpec(memory_space=pltpu.VMEM), pltpu.SemaphoreType.DMA
    return pl.pallas_call(
        kernel,
        out_shape=jax.ShapeDtypeStruct((4, ROWS, Y), F32),
        in_specs=[pl.BlockSpec(memory_space=pl.ANY)],
        out_specs=vmem,
        scratch_shapes=[
            pltpu.VMEM((Y + 256, Y), BF16),
            pltpu.VMEM((6 * ROWS, 256), BF16),
            pltpu.VMEM((2, 16, 128), BF16),
            pltpu.VMEM((2, 128, 16), BF16),
            pltpu.VMEM((Z + 4, X + 2 * EDGE, Y), BF16),
            pltpu.VMEM((2, DEPTH, ROWS, 128), BF16),
            pltpu.VMEM((2, DEPTH, ROWS, 128), BF16),
            pltpu.VMEM((2, 2 * Z, Y), BF16),
            pltpu.VMEM((2, 2 * Z, Y), BF16),
            pltpu.VMEM((DEPTH, 4, ROWS, Y), F32),
            pltpu.VMEM((DEPTH, 4, ROWS, Y), F32),
        ]
        + [dma((DEPTH,))]
        + [dma((2, DEPTH))] * 2
        + [dma((2,))] * 2
        + [dma((2, DEPTH))] * 2
        + [dma((DEPTH,))] * 2
        + [pltpu.VMEM((8, ROWS, Y), F32)] * 4
        + [pltpu.VMEM((3, 8, ROWS, Y), F32)] * 4,
        compiler_params=pltpu.CompilerParams(collective_id=0, has_side_effects=True, vmem_limit_bytes=48 << 20),
        name="render",
    )(density)


def solution(mesh):
    return jax.shard_map(
        on_device,
        mesh=mesh,
        in_specs=(P("depth", "ix", "iy"),),
        out_specs=P(None, ("ix", "depth"), "iy"),
        check_vma=False,
    )
```
